32 devices in a mesh: col: 4 (over z), rhs: 8 (over y, x, core).
Axes of the slice: x: 2, y: 2, z: 4, core: 2. Of those that a mesh axis runs over, the one named last changes fastest.
Arguments:
- desc_rows: bfloat16 [32, 1024, 1024], P(('col', 'rhs')), may hold values from -6 to 6
- upd_factor: bfloat16 [32, 1024, 1024], P(('col', 'rhs')), may hold values from -0.03125 to 0.03125
- update_index: int32 [32, 1024], P(('col', 'rhs')), may hold values from -1 to 1023, as said below
- owner_map: int32 [32, 4], P(('col', 'rhs')), may hold values from 0 to 3, each once within a row
- sep_rhs: float32 [1024, 4096], P('rhs', 'col'), may hold values from -6 to 6
- factor_rows: bfloat16 [4096, 4096], P('col'), may hold values from -0.046875 to 0.046875
- diag_inverse: bfloat16 [4096, 1024], P('col'), may hold values from -1 to 1
Outputs:
- solved: float32 [1024, 4096], P('rhs', 'col')
The draws below stay inside these ranges and needn't reach their ends.
Inputs may be any that keep to these rules, and one draw needn't show every extreme that they name: `update_index`: within each group of 256 slots of a descendant the live entries come first and are distinct rows of the block that owner_map names for that group; the other slots hold -1. Every descendant has at least one group with all 256 slots live.
All inputs are finite; a program needn't handle non-finite values.
Results may differ from the reference program's by a relative error of at most 0.004.
Values sent between devices are 32-bit elements; how exact they have to be, the bound alone decides.
No kernel may reach another device: no remote copies, remote signals or barrier semaphores. Data moves between devices by JAX's collectives and lax.ppermute only.
A program may use at most 128 MiB of HBM per device.

```python
import jax
import jax.numpy as jnp
from jax import lax

NB = 1024
CAP = 256
SEP = 4096
UPD = 1024
RHS_TOT = 1024
DESCS = 32
N_COL = 4


def draw_update_index(key, part):
    block_count = SEP // NB
    groups = DESCS * block_count
    group_keys = jax.random.split(key, groups)
    chosen = jax.vmap(lambda single: jax.random.permutation(single, NB)[:CAP])(group_keys)
    counts = jax.random.randint(jax.random.fold_in(key, 7), (DESCS, block_count), 1, CAP + 1)
    fullest = jax.random.randint(jax.random.fold_in(key, 11), (DESCS,), 0, block_count)
    counts = jnp.where(jnp.arange(block_count)[None, :] == fullest[:, None], CAP, counts)
    live_slots = jnp.arange(CAP)[None, None, :] < counts[:, :, None]
    result = jnp.where(live_slots, chosen.reshape(DESCS, block_count, CAP), -1)
    return result.reshape(DESCS, block_count * CAP).astype(jnp.int32)


def draw_diag_inverse(key, part):
    block_count = SEP // NB
    entries = jax.random.normal(key, (block_count, NB, NB), jnp.float32) * NB ** (-0.5)
    triangle = jnp.triu(entries, 1) + jnp.eye(NB, dtype=jnp.float32)[None, :, :]
    return triangle.reshape(block_count * NB, NB).astype(jnp.bfloat16)


def block_levels(key, shape, cuts, smallest, largest):
    loudness, own = 1.0, jax.random.fold_in(key, 6)
    for dim, parts in cuts:
        draws = jnp.exp(jax.random.uniform(jax.random.fold_in(own, dim), (parts,), jnp.float32, smallest / len(cuts), largest / len(cuts)))
        loudness = loudness * jnp.repeat(draws, shape[dim] // parts).reshape([-1 if axis == dim else 1 for axis in range(len(shape))])
    return loudness


def bell_draw(own_key, dims, scale, limit, shards=(), held_as=jnp.bfloat16):
    values = scale * jax.random.normal(own_key, dims, jnp.float32)
    if shards:
        values = values * block_levels(own_key, dims, shards, -0.22, 0.18)
    return jnp.clip(values, -limit, limit).astype(held_as)


def setup_inputs(seed: int = 0) -> dict:
    arg_keys = jax.random.split(jax.random.key(seed), 8)
    desc_rows = bell_draw(arg_keys[0], (DESCS, RHS_TOT, NB), 1.0, 6.0, ((0, 32),))
    upd_factor = bell_draw(arg_keys[1], (DESCS, NB, UPD), (32 * NB) ** -0.5, 0.03125, ((0, 32),))
    update_index = draw_update_index(jax.random.fold_in(arg_keys[7], 71), 0)
    owner_map = jax.vmap(lambda own: jax.random.permutation(own, N_COL))(jax.random.split(arg_keys[3], DESCS)).reshape((DESCS, N_COL)).astype(jnp.int32)
    sep_rhs = bell_draw(arg_keys[4], (RHS_TOT, SEP), 1.0, 6.0, ((0, 8), (1, 4)), jnp.float32)
    factor_rows = bell_draw(arg_keys[5], (SEP, SEP), (4 * SEP) ** -0.5, 0.046875, ((0, 4),))
    diag_inverse = draw_diag_inverse(jax.random.fold_in(arg_keys[7], 71), 0)
    return {"desc_rows": desc_rows, "upd_factor": upd_factor, "update_index": update_index, "owner_map": owner_map, "sep_rhs": sep_rhs, "factor_rows": factor_rows, "diag_inverse": diag_inverse}


def product(left, right):
    return jnp.dot(left.astype(jnp.float32), right.astype(jnp.float32),
                   precision=lax.Precision.HIGHEST, preferred_element_type=jnp.float32)


def reference(desc_rows, upd_factor, update_index, owner_map, sep_rhs, factor_rows, diag_inverse):
    def add_descendant(running, pieces):
        solved_rows, factor, local_index, owners = pieces
        update = product(solved_rows, factor)
        blocks = jnp.repeat(owners, CAP)
        targets = jnp.where(local_index >= 0, blocks * NB + local_index, SEP).astype(jnp.int32)
        return running.at[:, targets].add(update, mode="drop"), None

    assembled, _ = lax.scan(add_descendant, jnp.zeros((RHS_TOT, SEP), jnp.float32),
                            (desc_rows, upd_factor, update_index, owner_map))
    corrected = sep_rhs - assembled
    solved_blocks = []
    for column in range(N_COL):
        pending = jnp.zeros((RHS_TOT, NB), jnp.float32)
        for earlier in range(column):
            coupling = factor_rows[earlier * NB:(earlier + 1) * NB, column * NB:(column + 1) * NB]
            pending = pending + product(solved_blocks[earlier].astype(jnp.bfloat16), coupling)
        reduced = corrected[:, column * NB:(column + 1) * NB] - pending
        inverse_block = diag_inverse[column * NB:(column + 1) * NB]
        solved_blocks.append(product(reduced.astype(jnp.bfloat16), inverse_block))
    return jnp.concatenate(solved_blocks, axis=1)
```

```python
import functools

import jax
import jax.numpy as jnp
from jax import lax
from jax.experimental import pallas as pl
from jax.experimental.pallas import tpu as pltpu
from jax.sharding import PartitionSpec as P

PARAMS = pltpu.CompilerParams(vmem_limit_bytes=40 * 1024 * 1024)
INDEX_ROWS = 8
SOURCES = 4


def whole():
    return pl.BlockSpec(memory_space=pltpu.VMEM)


def contract(left, right):
    return jnp.dot(left, right, preferred_element_type=jnp.float32)


def group_of(owner_ref, block, count):
    found = jnp.int32(0)
    for place in range(count):
        found = found + jnp.where(owner_ref[0, place] == block, place, 0)
    return found


def payload_kernel(blocks, count, with_index, owner_ref, rows_ref, factor_ref, index_ref, out_ref):
    tiles, tile_rows, _ = rows_ref.shape
    capacity = factor_ref.shape[1] // count

    def window(block):
        return pl.ds(pl.multiple_of(group_of(owner_ref, block, count) * capacity, capacity), capacity)

    batch = min(4, tiles)
    for position, block in enumerate(blocks):
        factor = factor_ref[:, window(block)]

        def body(step, _, factor=factor, position=position):
            first = step * batch
            left = rows_ref[pl.ds(first, batch)].reshape(batch * tile_rows, -1)
            out_ref[pl.ds(first, batch), pl.ds(position * tile_rows, tile_rows), :] = contract(
                left, factor
            ).reshape(batch, tile_rows, capacity)
            return 0

        lax.fori_loop(0, tiles // batch, body, 0)
    if with_index:
        lists = [index_ref[:, window(block)] for block in range(count)]
        lists.append(jnp.full((INDEX_ROWS - count, capacity), -1, jnp.int32))
        table = jnp.concatenate(lists, axis=0).astype(jnp.float32)
        out_ref[:, pl.ds(len(blocks) * tile_rows, INDEX_ROWS), :] = jnp.broadcast_to(
            table[None], (tiles, INDEX_ROWS, capacity)
        )


def payload(blocks, with_index, owner, rows, factor, index, count):
    tiles, tile_rows, _ = rows.shape
    capacity = factor.shape[1] // count
    height = len(blocks) * tile_rows + (INDEX_ROWS if with_index else 0)
    return pl.pallas_call(
        functools.partial(payload_kernel, blocks, count, with_index),
        out_shape=jax.ShapeDtypeStruct((tiles, height, capacity), jnp.float32),
        in_specs=[pl.BlockSpec(memory_space=pltpu.SMEM), whole(), whole(), whole()],
        out_specs=whole(),
        compiler_params=PARAMS,
        cost_estimate=pl.CostEstimate(
            flops=2 * tiles * tile_rows * factor.shape[0] * capacity * len(blocks),
            bytes_accessed=4 * 1024 * 1024,
            transcendentals=0,
        ),
    )(owner, rows, factor, index)


def assemble_kernel(block, block_size, values_ref, index_ref, *outs):
    sources, tile_rows, capacity = values_ref.shape
    values = jnp.concatenate([values_ref[source] for source in range(sources)], axis=1)
    places = lax.broadcasted_iota(jnp.int32, (block_size, capacity), 0)
    spread = jnp.concatenate(
        [
            jnp.where(
                places == index_ref[source, pl.ds(block, 1), :].astype(jnp.int32), 1.0, 0.0
            ).astype(jnp.bfloat16)
            for source in range(sources)
        ],
        axis=1,
    )
    high = values.astype(jnp.bfloat16)
    low = (values - high.astype(jnp.float32)).astype(jnp.bfloat16)
    both = lax.dot_general(
        jnp.concatenate([high, low], axis=0),
        spread,
        (((1,), (1,)), ((), ())),
        preferred_element_type=jnp.float32,
    )
    total = both[:tile_rows] + both[tile_rows:]
    first = pl.program_id(0) == 0
    part_rows = tile_rows // len(outs)
    for part, out_ref in enumerate(outs):
        piece = total[part * part_rows : (part + 1) * part_rows]

        @pl.when(first)
        def _(out_ref=out_ref, piece=piece):
            out_ref[...] = piece

        @pl.when(jnp.logical_not(first))
        def _(out_ref=out_ref, piece=piece):
            out_ref[...] += piece


def assemble(block, position, arrived, index_holder, tile_rows, block_size, parts):
    tiles, _, capacity = arrived.shape
    index_place = index_holder.shape[1] // INDEX_ROWS - 1
    sources = min(SOURCES, tiles)
    part_rows = tile_rows // parts
    return pl.pallas_call(
        functools.partial(assemble_kernel, block, block_size),
        grid=(tiles // sources,),
        out_shape=[jax.ShapeDtypeStruct((part_rows, block_size), jnp.float32)] * parts,
        in_specs=[
            pl.BlockSpec((sources, tile_rows, capacity), lambda step: (step, position, 0)),
            pl.BlockSpec((sources, INDEX_ROWS, capacity), lambda step: (step, index_place, 0)),
        ],
        out_specs=[pl.BlockSpec((part_rows, block_size), lambda step: (0, 0))] * parts,
        compiler_params=PARAMS,
        cost_estimate=pl.CostEstimate(
            flops=4 * tiles * tile_rows * capacity * block_size,
            bytes_accessed=2 * 1024 * 1024,
            transcendentals=0,
        ),
    )(arrived, index_holder)


def station_kernel(station, terms, has_next, extra, held, *refs):
    refs = list(refs)
    right_ref = refs.pop(0)
    term_refs = [refs.pop(0) for _ in range(terms)]
    inverse_ref = refs.pop(0)
    if has_next:
        factor_ref = refs.pop(0)
        extra_refs = [refs.pop(0) for _ in range(extra)]
    held_refs = [refs.pop(0) for _ in range(held)]
    solved_ref = refs.pop(0)
    place = lax.axis_index("col")

    @pl.when(place == station)
    def _():
        reduced = right_ref[...]
        for term_ref in term_refs:
            reduced = reduced - term_ref[...]
        solved = contract(reduced.astype(jnp.bfloat16), inverse_ref[...])
        solved_ref[...] = solved
        if has_next:
            onward = contract(solved.astype(jnp.bfloat16), factor_ref[...])
            for extra_ref in extra_refs:
                onward = onward + extra_ref[...]
            refs[0][...] = onward

    for earlier, held_ref in enumerate(held_refs):

        @pl.when(place == earlier)
        def _(held_ref=held_ref):
            solved_ref[...] = held_ref[...]


def piece_spec(array, part, part_rows, width):
    if array.shape[0] == part_rows:
        return pl.BlockSpec((part_rows, width), lambda *_: (0, 0))
    return pl.BlockSpec((part_rows, width), lambda *_: (part, 0))


def station_step(station, part, parts, sep_rhs, terms, inverse, factor, extra, held):
    tile_rows, width = sep_rhs.shape
    part_rows = tile_rows // parts
    has_next = factor is not None
    rows = functools.partial(piece_spec, part=part, part_rows=part_rows, width=width)
    operands = [sep_rhs, *terms, inverse]
    specs = [rows(array) for array in (sep_rhs, *terms)]
    specs.append(pl.BlockSpec((inverse.shape[0], width), lambda *_: (0, 0)))
    if has_next:
        operands += [factor, *extra]
        specs.append(pl.BlockSpec((factor.shape[0], width), lambda *_: (0, station + 1)))
        specs += [rows(array) for array in extra]
    operands += held
    specs += [rows(array) for array in held]
    piece = jax.ShapeDtypeStruct((part_rows, width), jnp.float32)
    count = 2 if has_next else 1
    return pl.pallas_call(
        functools.partial(
            station_kernel, station, len(terms), has_next, len(extra), len(held)
        ),
        grid=(1,),
        out_shape=[piece] * count,
        in_specs=specs,
        out_specs=[pl.BlockSpec((part_rows, width), lambda *_: (0, 0))] * count,
        compiler_params=PARAMS,
        cost_estimate=pl.CostEstimate(
            flops=2 * count * part_rows * width * width,
            bytes_accessed=2 * count * width * width,
            transcendentals=0,
        ),
    )(*operands)


def onward_kernel(station, extra, solved_ref, factor_ref, *refs):
    @pl.when(lax.axis_index("col") == station)
    def _():
        onward = contract(solved_ref[...].astype(jnp.bfloat16), factor_ref[...])
        for extra_ref in refs[:extra]:
            onward = onward + extra_ref[...]
        refs[extra][...] = onward


def onward_step(station, block, part, parts, solved, factor, extra):
    part_rows, width = solved.shape
    rows = functools.partial(piece_spec, part=part, part_rows=part_rows, width=width)
    return pl.pallas_call(
        functools.partial(onward_kernel, station, len(extra)),
        grid=(1,),
        out_shape=jax.ShapeDtypeStruct((part_rows, width), jnp.float32),
        in_specs=[
            rows(solved),
            pl.BlockSpec((factor.shape[0], width), lambda *_: (0, block)),
            *[rows(array) for array in extra],
        ],
        out_specs=pl.BlockSpec((part_rows, width), lambda *_: (0, 0)),
        compiler_params=PARAMS,
        cost_estimate=pl.CostEstimate(
            flops=2 * part_rows * width * width,
            bytes_accessed=2 * width * width,
            transcendentals=0,
        ),
    )(solved, factor, *extra)


def exchange(value):
    return lax.all_to_all(value, "rhs", split_axis=0, concat_axis=0, tiled=True)


def moved(value, pairs):
    return lax.ppermute(value, "col", pairs)


def local(desc_rows, upd_factor, update_index, owner_map, sep_rhs, factor_rows, diag_inverse):
    count = lax.axis_size("col")
    tiles = lax.axis_size("rhs")
    block_size = diag_inverse.shape[0]
    tile_rows = sep_rhs.shape[0]
    parts = PARTS
    rows = desc_rows[0].reshape(tiles, tile_rows, block_size)
    make = functools.partial(
        payload, owner=owner_map, rows=rows, factor=upd_factor[0], index=update_index, count=count
    )
    first = exchange(make((0,), True))
    partial = {0: assemble(0, 0, first, first, tile_rows, block_size, parts)}
    for blocks in GROUPS:
        arrived = exchange(make(blocks, False))
        for position, block in enumerate(blocks):
            partial[block] = assemble(block, position, arrived, first, tile_rows, block_size, 1)

    gathered = {}
    for part in range(parts):
        stride, terms, value = 1, [partial[0][part]], partial[0][part]
        while stride < count:
            pairs = [(place + stride, place) for place in range(0, count - stride, 2 * stride)]
            received = moved(value, pairs)
            terms.append(received)
            stride *= 2
            if stride < count:
                value = value + received
        gathered[0, part] = terms
    for block in range(1, count):
        value = partial[block][0]
        received = None
        for source in range(count - 1, block, -1):
            sent = value if received is None else value + received
            received = moved(sent, [(source, source - 1)])
        for part in range(parts):
            gathered[block, part] = [value] + ([] if received is None else [received])

    held = {part: [] for part in range(parts)}
    for station in range(count):
        last = station + 1 == count
        for part in range(parts):
            outs = station_step(
                station, part, parts, sep_rhs, gathered[station, part], diag_inverse,
                None if last else factor_rows,
                [] if last else [partial[station + 1][0]],
                held[part] if last else [],
            )
            held[part].append(outs[0])
            if not last:
                gathered[station + 1, part].append(moved(outs[1], [(station, station + 1)]))
        for block in range(station + 2, count):
            for part in range(parts):
                onward = onward_step(
                    station, block, part, parts, held[part][station], factor_rows,
                    [partial[block][0]],
                )
                gathered[block, part].append(moved(onward, [(station, block)]))
    return jnp.concatenate([held[part][-1] for part in range(parts)], axis=0)


PARTS = 2
GROUPS = ((1,), (2, 3))


def solution(mesh):
    placed = (
        P(("col", "rhs"), None, None),
        P(("col", "rhs"), None, None),
        P(("col", "rhs"), None),
        P(("col", "rhs"), None),
        P("rhs", "col"),
        P("col", None),
        P("col", None),
    )
    return jax.shard_map(
        local, mesh=mesh, in_specs=placed, out_specs=P("rhs", "col"), check_vma=False
    )
```

```python
import functools

import jax
import jax.numpy as jnp
from jax import lax
from jax.experimental import pallas as pl
from jax.experimental.pallas import tpu as pltpu
from jax.sharding import PartitionSpec as P

MIB = 1024 * 1024
CORES = 2
INDEX_ROWS = 8
SOURCES = 4
PARTS = 1


def params(mib):
    return pltpu.CompilerParams(vmem_limit_bytes=mib * MIB)


def cost(flops, bytes_accessed):
    return pl.CostEstimate(flops=0, bytes_accessed=0, transcendentals=0)


def in_vmem():
    return pl.BlockSpec(memory_space=pltpu.VMEM)


def in_hbm():
    return pl.BlockSpec(memory_space=pltpu.HBM)


def after(values, earlier):
    values, earlier = tuple(values), tuple(earlier)
    return lax.optimization_barrier(values + earlier)[: len(values)]


def contract(left, right):
    return jnp.dot(left, right, preferred_element_type=jnp.float32)


def group_of(owner_ref, block, count):
    found = jnp.int32(0)
    for place in range(count):
        found = found + jnp.where(owner_ref[0, place] == block, place, 0)
    return found


def payload_kernel(blocks, count, with_index, owner_ref, rows_ref, factor_ref, index_ref, *outs):
    tiles, tile_rows, _ = rows_ref.shape
    chips = tiles // CORES
    capacity = factor_ref.shape[1] // count
    own = lax.axis_index("rhs")
    chip, core = lax.div(own, CORES), lax.rem(own, CORES)

    def window(block):
        return pl.ds(pl.multiple_of(group_of(owner_ref, block, count) * capacity, capacity), capacity)

    for position, block in enumerate(blocks):
        factor = factor_ref[:, window(block)]
        for offset in range(chips):
            target = jnp.bitwise_xor(chip, offset) * CORES
            left = jnp.concatenate(
                [rows_ref[target + core], rows_ref[target + (CORES - 1) - core]], axis=0
            )
            outs[position * chips + offset][: CORES * tile_rows, :] = contract(left, factor)
    if with_index:
        lists = [index_ref[:, window(block)] for block in range(count)]
        lists.append(jnp.full((INDEX_ROWS - count, capacity), -1, jnp.int32))
        table = jnp.concatenate(lists, axis=0).astype(jnp.float32)
        for out_ref in outs:
            out_ref[CORES * tile_rows :, :] = table


def payload(blocks, with_index, owner, rows, factor, index, count):
    tiles, tile_rows, depth = rows.shape
    chips = tiles // CORES
    capacity = factor.shape[1] // count
    height = CORES * tile_rows + (INDEX_ROWS if with_index else 0)
    piece = jax.ShapeDtypeStruct((height, capacity), jnp.float32)
    outs = pl.pallas_call(
        functools.partial(payload_kernel, blocks, count, with_index),
        out_shape=[piece] * (chips * len(blocks)),
        in_specs=[pl.BlockSpec(memory_space=pltpu.SMEM), in_vmem(), in_vmem(), in_vmem()],
        out_specs=[in_vmem()] * (chips * len(blocks)),
        compiler_params=params(32),
        cost_estimate=cost(2 * tiles * tile_rows * depth * capacity * len(blocks), 4 * MIB),
    )(owner, rows, factor, index)
    return [outs[position * chips : (position + 1) * chips] for position in range(len(blocks))]


def assemble_kernel(block, block_size, tile_rows, chips, *refs):
    values_refs, index_refs, outs = refs[:chips], refs[chips : 2 * chips], refs[2 * chips :]
    capacity = values_refs[0].shape[1]
    height = CORES * tile_rows
    places = lax.broadcasted_iota(jnp.int32, (block_size, capacity), 0)
    total = None
    for first in range(0, chips, SOURCES):
        chosen = range(first, min(chips, first + SOURCES))
        values = jnp.concatenate([values_refs[chip][:height, :] for chip in chosen], axis=1)
        spread = jnp.concatenate(
            [
                jnp.where(
                    places
                    == index_refs[chip][pl.ds(height + block, 1), :].astype(jnp.int32),
                    1.0,
                    0.0,
                ).astype(jnp.bfloat16)
                for chip in chosen
            ],
            axis=1,
        )
        high = values.astype(jnp.bfloat16)
        low = (values - high.astype(jnp.float32)).astype(jnp.bfloat16)
        both = lax.dot_general(
            jnp.concatenate([high, low], axis=0),
            spread,
            (((1,), (1,)), ((), ())),
            preferred_element_type=jnp.float32,
        )
        both = both[:height] + both[height:]
        total = both if total is None else total + both
    outs[0][...] = total[:tile_rows]
    outs[1][...] = total[tile_rows:]


def assemble(block, arrived, holders, tile_rows, block_size):
    chips = len(arrived)
    capacity = arrived[0].shape[1]
    piece = jax.ShapeDtypeStruct((tile_rows, block_size), jnp.float32)
    return pl.pallas_call(
        functools.partial(assemble_kernel, block, block_size, tile_rows, chips),
        out_shape=[piece] * CORES,
        in_specs=[in_vmem()] * (2 * chips),
        out_specs=[in_vmem()] * CORES,
        compiler_params=params(24),
        cost_estimate=cost(4 * CORES * chips * tile_rows * capacity * block_size, 2 * MIB),
    )(*arrived, *holders)


def stage_kernel(factor_ref, inverse_ref, *refs):
    outs, semaphores = refs[:-1], refs[-1]
    width = inverse_ref.shape[1]
    sources = [inverse_ref] + [
        factor_ref.at[:, pl.ds(block * width, width)] for block in range(1, len(outs))
    ]
    copies = [
        pltpu.make_async_copy(source, out, semaphores.at[place])
        for place, (source, out) in enumerate(zip(sources, outs))
    ]
    for copy in copies:
        copy.start()
    for copy in copies:
        copy.wait()


def stage(factor, inverse, count):
    depth, width = inverse.shape
    piece = jax.ShapeDtypeStruct((depth, width), inverse.dtype)
    return pl.pallas_call(
        stage_kernel,
        out_shape=[piece] * count,
        in_specs=[in_hbm()] * 2,
        out_specs=[in_vmem()] * count,
        scratch_shapes=[pltpu.SemaphoreType.DMA((count,))],
        compiler_params=params(16),
        cost_estimate=cost(0, 16 * MIB),
    )(factor, inverse)


def rows_of(ref, part, part_rows):
    if ref.shape[0] == part_rows:
        return ref[...]
    return ref[pl.ds(part * part_rows, part_rows), :]


def station_kernel(station, part, terms, has_next, extra, held, right_ref, inverse_ref, *refs):
    refs = list(refs)
    term_refs = [refs.pop(0) for _ in range(terms)]
    factor_ref = refs.pop(0) if has_next else None
    extra_refs = [refs.pop(0) for _ in range(extra)]
    held_refs = [refs.pop(0) for _ in range(held)]
    solved_ref = refs.pop(0)
    part_rows = solved_ref.shape[0]
    place = lax.axis_index("col")

    @pl.when(place == station)
    def _():
        reduced = rows_of(right_ref, part, part_rows)
        for term_ref in term_refs:
            reduced = reduced - rows_of(term_ref, part, part_rows)
        solved = contract(reduced.astype(jnp.bfloat16), inverse_ref[...])
        solved_ref[...] = solved
        if has_next:
            onward = contract(solved.astype(jnp.bfloat16), factor_ref[...])
            for extra_ref in extra_refs:
                onward = onward + rows_of(extra_ref, part, part_rows)
            refs[0][...] = onward

    for earlier, held_ref in enumerate(held_refs):

        @pl.when(place == earlier)
        def _(held_ref=held_ref):
            solved_ref[...] = held_ref[...]


def station_step(station, part, right, inverse, terms, factor, extra, held):
    part_rows, width = right.shape[0] // PARTS, right.shape[1]
    operands = [right, inverse, *terms, *([] if factor is None else [factor]), *extra, *held]
    piece = jax.ShapeDtypeStruct((part_rows, width), jnp.float32)
    count = 1 if factor is None else 2
    return pl.pallas_call(
        functools.partial(
            station_kernel, station, part, len(terms), factor is not None, len(extra), len(held)
        ),
        out_shape=[piece] * count,
        in_specs=[in_vmem()] * len(operands),
        out_specs=[in_vmem()] * count,
        compiler_params=params(16),
        cost_estimate=cost(2 * count * part_rows * width * width, 2 * MIB),
    )(*operands)


def onward_kernel(station, part, solved_ref, factor_ref, *refs):
    @pl.when(lax.axis_index("col") == station)
    def _():
        onward = contract(solved_ref[...].astype(jnp.bfloat16), factor_ref[...])
        for extra_ref in refs[:-1]:
            onward = onward + rows_of(extra_ref, part, onward.shape[0])
        refs[-1][...] = onward


def onward_step(station, part, solved, factor, extra):
    part_rows, width = solved.shape
    return pl.pallas_call(
        functools.partial(onward_kernel, station, part),
        out_shape=jax.ShapeDtypeStruct((part_rows, width), jnp.float32),
        in_specs=[in_vmem()] * (2 + len(extra)),
        out_specs=in_vmem(),
        compiler_params=params(16),
        cost_estimate=cost(2 * part_rows * width * width, 2 * MIB),
    )(solved, factor, *extra)


def local(desc_rows, upd_factor, update_index, owner_map, sep_rhs, factor_rows, diag_inverse):
    count = lax.axis_size("col")
    tiles = lax.axis_size("rhs")
    chips = tiles // CORES
    block_size = diag_inverse.shape[0]
    tile_rows = sep_rhs.shape[0]
    part_rows = tile_rows // PARTS
    parts = range(PARTS)

    def across(value, offset):
        pairs = [(place, place ^ (offset * CORES)) for place in range(tiles)]
        return lax.ppermute(value, "rhs", pairs)

    def other_core(value):
        return lax.ppermute(value, "rhs", [(place, place ^ 1) for place in range(tiles)])

    def moved(value, pairs):
        return lax.ppermute(value, "col", pairs)

    token = []

    def ordered(values):
        return list(after(values, token)) if token else list(values)

    def done_with(value):
        token[:] = [value]

    rows = desc_rows[0].reshape(tiles, tile_rows, block_size)
    make = functools.partial(
        payload, owner=owner_map, factor=upd_factor[0], index=update_index, count=count
    )
    first_payload = make((0,), True, rows=rows)[0]
    done_with(first_payload[0])
    rest = make(tuple(range(1, count)), False, rows=ordered([rows])[0])
    payloads = [first_payload, *rest]
    done_with(rest[0][0])
    weights = stage(*ordered([factor_rows, diag_inverse]), count)
    inverse, couplings = weights[0], weights[1:]
    done_with(inverse)

    arriving = {}

    def send_block(block, gates):
        sent = payloads[block]
        pieces = [sent[0]]
        for offset in range(1, chips):
            value = sent[offset]
            if gates is not None:
                value = after([value], [gates[offset]])[0]
            pieces.append(across(value, offset))
        arriving[block] = pieces

    partial = {}
    terms = {block: [[] for _ in parts] for block in range(count)}

    crossing = {}

    def assemble_block(block):
        values = ordered(arriving[block])
        mine, other = assemble(block, values, arriving[0], tile_rows, block_size)
        done_with(mine)
        if block + 1 < count:
            gate = other if block == 0 else terms[0][-1][min(block, len(terms[0][-1]) - 1)]
            send_block(block + 1, [gate] * chips)
        crossing[block] = (mine, other_core(other))

    def close_block(block):
        partial[block] = []
        for part in parts:
            mine, received = ordered(crossing[block])
            window = slice(part * part_rows, (part + 1) * part_rows)
            partial[block].append(mine[window] + received[window])
            done_with(partial[block][-1])

    flows, pending = {}, {}

    def hops_of(block):
        hops, stride = [], 1
        if block == 0:
            while stride < count:
                hops.append([(p + stride, p) for p in range(0, count - stride, 2 * stride)])
                stride *= 2
        else:
            hops = [[(p, p - 1)] for p in range(count - 1, block, -1)]
        return hops

    def start_flow(block):
        flows[block] = [hops_of(block), list(partial[block])]
        for part in parts:
            terms[block][part].append(partial[block][part])
        hop(block)

    def hop(block, chosen=parts):
        hops, values = flows[block]
        if not hops:
            return
        for part in chosen:
            if (block, part) in pending:
                base, received = ordered(pending.pop((block, part)))
                values[part] = base + received
                done_with(values[part])
            received = moved(values[part], hops[0])
            if block == 0 or len(hops) == 1:
                terms[block][part].append(received)
            pending[block, part] = (values[part] if block == 0 else partial[block][part], received)
        if PARTS - 1 in chosen:
            hops.pop(0)

    held = {part: [] for part in parts}

    def solve(station):
        last = station + 1 == count
        for part in parts:
            extra = [] if last else [partial[station + 1][part]]
            wanted = ordered(terms[station][part])
            outs = station_step(
                station, part, sep_rhs, inverse, wanted, None if last else couplings[station],
                extra, held[part] if last else [],
            )
            done_with(outs[0])
            held[part].append(outs[0])
            if not last:
                terms[station + 1][part].append(moved(outs[1], [(station, station + 1)]))

    def pass_on(station, block):
        for part in parts:
            solved = ordered([held[part][station]])[0]
            value = onward_step(
                station, part, solved, couplings[block - 1], [partial[block][part]]
            )
            done_with(value)
            terms[block][part].append(moved(value, [(station, block)]))

    passed = set()

    def pass_ready(station, block):
        for earlier in range(min(station + 1, block - 1)):
            if (earlier, block) not in passed:
                passed.add((earlier, block))
                pass_on(earlier, block)

    send_block(0, None)
    following = 0
    for block in range(count):
        if following < block and not flows[following][0]:
            solve(following)
            following += 1
        if block:
            hop(0, parts[:1])
        assemble_block(block)
        if block:
            hop(0, parts[1:])
        for earlier in range(1, block):
            hop(earlier)
        close_block(block)
        for later in range(2, block + 1):
            pass_ready(following - 1, later)
        start_flow(block)
    for station in range(following, count):
        pass_ready(station - 1, station)
        solve(station)
    return jnp.concatenate([held[part][-1] for part in parts], axis=0)


def solution(mesh):
    placed = (
        P(("col", "rhs"), None, None),
        P(("col", "rhs"), None, None),
        P(("col", "rhs"), None),
        P(("col", "rhs"), None),
        P("rhs", "col"),
        P("col", None),
        P("col", None),
    )
    return jax.shard_map(
        local, mesh=mesh, in_specs=placed, out_specs=P("rhs", "col"), check_vma=False
    )
```

```python
import functools

import jax
import jax.numpy as jnp
from jax import lax
from jax.experimental import pallas as pl
from jax.experimental.pallas import tpu as pltpu
from jax.sharding import PartitionSpec as P

MIB = 1024 * 1024
CORES = 2
INDEX_ROWS = 8
SOURCES = 4
PARTS = 2


def params(mib):
    return pltpu.CompilerParams(vmem_limit_bytes=mib * MIB)


def cost(flops, bytes_accessed):
    return pl.CostEstimate(flops=0, bytes_accessed=0, transcendentals=0)


def in_vmem():
    return pl.BlockSpec(memory_space=pltpu.VMEM)


def in_hbm():
    return pl.BlockSpec(memory_space=pltpu.HBM)


def after(values, earlier):
    values, earlier = tuple(values), tuple(earlier)
    return lax.optimization_barrier(values + earlier)[: len(values)]


def contract(left, right):
    return jnp.dot(left, right, preferred_element_type=jnp.float32)


def group_of(owner_ref, block, count):
    found = jnp.int32(0)
    for place in range(count):
        found = found + jnp.where(owner_ref[0, place] == block, place, 0)
    return found


def payload_kernel(blocks, parts, count, with_index, owner_ref, rows_ref, factor_ref, index_ref, *refs):
    outs, (rows_held, factor_held, semaphores) = refs[:-3], refs[-3:]
    tiles, tile_rows, _ = rows_ref.shape
    chips = tiles // CORES
    part_rows = tile_rows // parts
    capacity = factor_ref.shape[1] // count
    own = lax.axis_index("rhs")
    chip, core = lax.div(own, CORES), lax.rem(own, CORES)

    def window(block):
        return pl.ds(pl.multiple_of(group_of(owner_ref, block, count) * capacity, capacity), capacity)

    def target(offset):
        return jnp.bitwise_xor(chip, offset) * CORES

    copies = [
        pltpu.make_async_copy(
            factor_ref.at[:, window(block)], factor_held.at[position], semaphores.at[position]
        )
        for position, block in enumerate(blocks)
    ]
    for offset in range(chips):
        place = pl.ds(target(offset), CORES)
        copies.append(
            pltpu.make_async_copy(
                rows_ref.at[place], rows_held.at[place], semaphores.at[len(blocks) + offset]
            )
        )
    for copy in copies:
        copy.start()
    if with_index:
        lists = [index_ref[:, window(block)] for block in range(count)]
        lists.append(jnp.full((INDEX_ROWS - count, capacity), -1, jnp.int32))
        table = jnp.concatenate(lists, axis=0).astype(jnp.float32)
        for out_ref in outs[:CORES]:
            for offset in range(chips):
                out_ref[0, offset, part_rows:, :] = table
    for position in range(len(blocks)):
        copies[position].wait()
        for offset in range(chips):
            if position == 0:
                copies[len(blocks) + offset].wait()
            left = jnp.concatenate(
                [
                    rows_held[target(offset) + core],
                    rows_held[target(offset) + (CORES - 1) - core],
                ],
                axis=0,
            )
            product = contract(left, factor_held[position])
            for part in range(parts):
                for side in range(CORES):
                    begin = side * tile_rows + part * part_rows
                    outs[part * CORES + side][position, offset, :part_rows, :] = product[
                        begin : begin + part_rows
                    ]


def payload(blocks, parts, with_index, owner, rows, factor, index, count):
    tiles, tile_rows, depth = rows.shape
    chips = tiles // CORES
    capacity = factor.shape[1] // count
    height = tile_rows // parts
    pieces = []
    for part in range(parts):
        extra = INDEX_ROWS if with_index and part == 0 else 0
        piece = jax.ShapeDtypeStruct((len(blocks), chips, height + extra, capacity), jnp.float32)
        pieces += [piece] * CORES
    return pl.pallas_call(
        functools.partial(payload_kernel, blocks, parts, count, with_index),
        name=f"payload_block{blocks[0]}",
        out_shape=pieces,
        in_specs=[pl.BlockSpec(memory_space=pltpu.SMEM), in_hbm(), in_hbm(), in_vmem()],
        out_specs=[in_vmem()] * len(pieces),
        scratch_shapes=[
            pltpu.VMEM(rows.shape, rows.dtype),
            pltpu.VMEM((len(blocks), depth, capacity), factor.dtype),
            pltpu.SemaphoreType.DMA((len(blocks) + chips,)),
        ],
        compiler_params=params(40),
        cost_estimate=cost(2 * tiles * tile_rows * depth * capacity * len(blocks), 4 * MIB),
    )(owner, rows, factor, index)


def assemble_kernel(block, block_size, height, chips, *refs):
    values_refs, index_refs, outs = refs[:chips], refs[chips : 2 * chips], refs[2 * chips :]
    capacity = values_refs[0].shape[2]
    index_row = index_refs[0].shape[1] - INDEX_ROWS + block
    places = lax.broadcasted_iota(jnp.int32, (block_size, capacity), 0)
    sources = [(chip, core) for chip in range(chips) for core in range(CORES)]
    total = None
    for first in range(0, len(sources), SOURCES):
        chosen = sources[first : first + SOURCES]
        values = jnp.concatenate(
            [values_refs[chip][core, :height, :] for chip, core in chosen], axis=1
        )
        spread = jnp.concatenate(
            [
                jnp.where(
                    places == index_refs[chip][core, pl.ds(index_row, 1), :].astype(jnp.int32),
                    1.0,
                    0.0,
                ).astype(jnp.bfloat16)
                for chip, core in chosen
            ],
            axis=1,
        )
        high = values.astype(jnp.bfloat16)
        low = (values - high.astype(jnp.float32)).astype(jnp.bfloat16)
        both = lax.dot_general(
            jnp.concatenate([high, low], axis=0),
            spread,
            (((1,), (1,)), ((), ())),
            preferred_element_type=jnp.float32,
        )
        both = both[:height] + both[height:]
        total = both if total is None else total + both
    part_rows = height // len(outs)
    for part, out_ref in enumerate(outs):
        out_ref[...] = total[part * part_rows : (part + 1) * part_rows]


def assemble(block, arrived, holders, height, parts, block_size):
    chips = len(arrived)
    capacity = arrived[0].shape[2]
    piece = jax.ShapeDtypeStruct((height // parts, block_size), jnp.float32)
    return pl.pallas_call(
        functools.partial(assemble_kernel, block, block_size, height, chips),
        name=f"assemble_block{block}",
        out_shape=[piece] * parts,
        in_specs=[in_vmem()] * (2 * chips),
        out_specs=[in_vmem()] * parts,
        compiler_params=params(24),
        cost_estimate=cost(4 * CORES * chips * height * capacity * block_size, 2 * MIB),
    )(*arrived, *holders)


def stage_kernel(factor_ref, inverse_ref, *refs):
    outs, semaphores = refs[:-1], refs[-1]
    width = inverse_ref.shape[1]
    sources = [inverse_ref] + [
        factor_ref.at[:, pl.ds(block * width, width)] for block in range(1, len(outs))
    ]
    copies = [
        pltpu.make_async_copy(source, out, semaphores.at[place])
        for place, (source, out) in enumerate(zip(sources, outs))
    ]
    for copy in copies:
        copy.start()
    for copy in copies:
        copy.wait()


def stage(factor, inverse, count):
    depth, width = inverse.shape
    piece = jax.ShapeDtypeStruct((depth, width), inverse.dtype)
    return pl.pallas_call(
        stage_kernel,
        name="stage",
        out_shape=[piece] * count,
        in_specs=[in_hbm()] * 2,
        out_specs=[in_vmem()] * count,
        scratch_shapes=[pltpu.SemaphoreType.DMA((count,))],
        compiler_params=params(16),
        cost_estimate=cost(0, 16 * MIB),
    )(factor, inverse)


def rows_of(ref, part, part_rows):
    if ref.shape[0] == part_rows:
        return ref[...]
    return ref[pl.ds(part * part_rows, part_rows), :]


def station_kernel(station, part, terms, has_next, extra, held, right_ref, inverse_ref, *refs):
    refs = list(refs)
    term_refs = [refs.pop(0) for _ in range(terms)]
    factor_ref = refs.pop(0) if has_next else None
    extra_refs = [refs.pop(0) for _ in range(extra)]
    held_refs = [refs.pop(0) for _ in range(held)]
    solved_ref = refs.pop(0)
    part_rows = solved_ref.shape[0]
    place = lax.axis_index("col")

    @pl.when(place == station)
    def _():
        reduced = rows_of(right_ref, part, part_rows)
        for term_ref in term_refs:
            reduced = reduced - rows_of(term_ref, part, part_rows)
        solved = contract(reduced.astype(jnp.bfloat16), inverse_ref[...])
        solved_ref[...] = solved
        if has_next:
            onward = contract(solved.astype(jnp.bfloat16), factor_ref[...])
            for extra_ref in extra_refs:
                onward = onward + rows_of(extra_ref, part, part_rows)
            refs[0][...] = onward

    for earlier, held_ref in enumerate(held_refs):

        @pl.when(place == earlier)
        def _(held_ref=held_ref):
            solved_ref[...] = held_ref[...]


def station_step(station, part, right, inverse, terms, factor, extra, held):
    part_rows, width = right.shape[0] // PARTS, right.shape[1]
    operands = [right, inverse, *terms, *([] if factor is None else [factor]), *extra, *held]
    piece = jax.ShapeDtypeStruct((part_rows, width), jnp.float32)
    count = 1 if factor is None else 2
    return pl.pallas_call(
        functools.partial(
            station_kernel, station, part, len(terms), factor is not None, len(extra), len(held)
        ),
        name=f"solve{station}_part{part}",
        out_shape=[piece] * count,
        in_specs=[in_vmem()] * len(operands),
        out_specs=[in_vmem()] * count,
        compiler_params=params(16),
        cost_estimate=cost(2 * count * part_rows * width * width, 2 * MIB),
    )(*operands)


def onward_kernel(station, part, solved_ref, factor_ref, *refs):
    @pl.when(lax.axis_index("col") == station)
    def _():
        onward = contract(solved_ref[...].astype(jnp.bfloat16), factor_ref[...])
        for extra_ref in refs[:-1]:
            onward = onward + rows_of(extra_ref, part, onward.shape[0])
        refs[-1][...] = onward


def onward_step(station, part, solved, factor, extra):
    part_rows, width = solved.shape
    return pl.pallas_call(
        functools.partial(onward_kernel, station, part),
        name=f"onward{station}_part{part}",
        out_shape=jax.ShapeDtypeStruct((part_rows, width), jnp.float32),
        in_specs=[in_vmem()] * (2 + len(extra)),
        out_specs=in_vmem(),
        compiler_params=params(16),
        cost_estimate=cost(2 * part_rows * width * width, 2 * MIB),
    )(solved, factor, *extra)


def local(desc_rows, upd_factor, update_index, owner_map, sep_rhs, factor_rows, diag_inverse):
    count = lax.axis_size("col")
    tiles = lax.axis_size("rhs")
    chips = tiles // CORES
    block_size = diag_inverse.shape[0]
    tile_rows = sep_rhs.shape[0]
    part_rows = tile_rows // PARTS
    parts = range(PARTS)

    def across(value, offset):
        pairs = [(place, place ^ (offset * CORES)) for place in range(tiles)]
        return lax.ppermute(value, "rhs", pairs)

    def other_core(value):
        return lax.ppermute(value, "rhs", [(place, place ^ 1) for place in range(tiles)])

    def moved(value, pairs):
        return lax.ppermute(value, "col", pairs)

    token = []

    def ordered(values):
        return list(after(values, token)) if token else list(values)

    def done_with(value):
        token[:] = [value]

    rows = desc_rows[0].reshape(tiles, tile_rows, block_size)
    make = functools.partial(
        payload, owner=owner_map, factor=upd_factor[0], index=update_index, count=count
    )

    def both_cores(mine, other, name):
        with jax.named_scope(f"cores_{name}"):
            received = other_core(other)
        return [jnp.stack([mine[offset], received[offset]]) for offset in range(chips)]

    def send(pieces, gate, name):
        arrived = [pieces[0]]
        for offset in range(1, chips):
            value = pieces[offset]
            if gate is not None:
                value = after([value], [gate])[0]
            with jax.named_scope(f"plane{offset}_{name}"):
                arrived.append(across(value, offset))
        return arrived

    partial = {0: []}
    terms = {block: [[] for _ in parts] for block in range(count)}
    made = make((0,), PARTS, True, rows=rows)
    ready = [
        both_cores(made[part * CORES][0], made[part * CORES + 1][0], f"block0_part{part}")
        for part in parts
    ]
    done_with(ready[0][0])
    arrivals = [send(ready[0], None, "block0_part0")]
    made = make(tuple(range(1, count)), 1, False, rows=ordered([rows])[0])
    done_with(made[0])
    weights = stage(*ordered([factor_rows, diag_inverse]), count)
    inverse, couplings = weights[0], weights[1:]
    done_with(inverse)
    payloads = [
        both_cores(made[0][position], made[1][position], f"block{position + 1}")
        for position in range(count - 1)
    ]
    token += [pieces[0] for pieces in payloads]
    token += [pieces[0] for pieces in ready[1:]]
    for part in parts:
        if part:
            arrivals.append(send(ready[part], arrivals[-1][1], f"block0_part{part}"))
        values = ordered(arrivals[part])
        partial[0] += assemble(0, values, arrivals[0], part_rows, 1, block_size)
        done_with(partial[0][part])
    holders = arrivals[0]
    arriving = {1: send(payloads[0], arrivals[-1][1], "block1")}

    def assemble_block(block):
        values = ordered(arriving[block])
        partial[block] = assemble(block, values, holders, tile_rows, PARTS, block_size)
        done_with(partial[block][0])
        if block + 1 < count:
            arriving[block + 1] = send(payloads[block], arriving[block][1], f"block{block + 1}")

    flows, pending = {}, {}

    def hops_of(block):
        hops, stride = [], 1
        if block == 0:
            while stride < count:
                hops.append([(p + stride, p) for p in range(0, count - stride, 2 * stride)])
                stride *= 2
        else:
            hops = [[(p, p - 1)] for p in range(count - 1, block, -1)]
        return hops

    def start_flow(block):
        flows[block] = [hops_of(block), list(partial[block])]
        for part in parts:
            terms[block][part].append(partial[block][part])
        hop(block)

    def hop(block, chosen=parts):
        hops, values = flows[block]
        if not hops:
            return
        for part in chosen:
            if (block, part) in pending:
                base, received = ordered(pending.pop((block, part)))
                with jax.named_scope(f"relay_block{block}_part{part}"):
                    values[part] = base + received
                done_with(values[part])
            with jax.named_scope(f"down_block{block}_part{part}_left{len(hops)}"):
                received = moved(values[part], hops[0])
            if block == 0 or len(hops) == 1:
                terms[block][part].append(received)
            pending[block, part] = (values[part] if block == 0 else partial[block][part], received)
        if PARTS - 1 in chosen:
            hops.pop(0)

    held = {part: [] for part in parts}

    def solve(station):
        last = station + 1 == count
        for part in parts:
            extra = [] if last else [partial[station + 1][part]]
            wanted = ordered(terms[station][part])
            outs = station_step(
                station, part, sep_rhs, inverse, wanted, None if last else couplings[station],
                extra, held[part] if last else [],
            )
            done_with(outs[0])
            held[part].append(outs[0])
            if not last:
                with jax.named_scope(f"up_from{station}_block{station + 1}_part{part}"):
                    terms[station + 1][part].append(moved(outs[1], [(station, station + 1)]))

    relayed = {}

    def pass_on(station, block):
        onto = block if station + 2 == block else station + 1
        for part in parts:
            solved = ordered([held[part][station]])[0]
            extra = [partial[block][part]]
            if (block, part) in relayed:
                extra.append(relayed.pop((block, part)))
            value = onward_step(station, part, solved, couplings[block - 1], extra)
            done_with(value)
            with jax.named_scope(f"up_from{station}_block{block}_part{part}"):
                received = moved(value, [(station, onto)])
            if onto == block:
                terms[block][part].append(received)
            else:
                relayed[block, part] = received

    passed = set()

    def pass_ready(station, block):
        for earlier in range(min(station + 1, following, block - 1)):
            if (earlier, block) not in passed:
                passed.add((earlier, block))
                pass_on(earlier, block)

    start_flow(0)
    following = 0
    for block in range(1, count):
        for earlier in range(block):
            hop(earlier)
        assemble_block(block)
        start_flow(block)
        if following < block and not flows[following][0]:
            pass_ready(max(following - 2, 0), block)
            pass_ready(following - 1, following)
            solve(following)
            following += 1
    for station in range(following, count):
        pass_ready(station - 1, station)
        solve(station)
    return jnp.concatenate([held[part][-1] for part in parts], axis=0)


def solution(mesh):
    placed = (
        P(("col", "rhs"), None, None),
        P(("col", "rhs"), None, None),
        P(("col", "rhs"), None),
        P(("col", "rhs"), None),
        P("rhs", "col"),
        P("col", None),
        P("col", None),
    )
    return jax.shard_map(
        local, mesh=mesh, in_specs=placed, out_specs=P("rhs", "col"), check_vma=False
    )
```

```python
import functools

import jax
import jax.numpy as jnp
from jax import lax
from jax.experimental import pallas as pl
from jax.experimental.pallas import tpu as pltpu
from jax.sharding import PartitionSpec as P

MIB = 1024 * 1024
STAGE, PAYLOAD, ASSEMBLE, RELAY, SOLVE, PASS, PLANE, DOWN, UP = range(9)
CORES = 2
INDEX_ROWS = 8
SOURCES = 4
PARTS = 2
BATCH = 4
FIRST_MIB, REST_MIB = 52, 40
FLOW_PARTS = (2, 1, 1, 1)
ORDER = (
    (RELAY, 0, 1, 0),
    (ASSEMBLE, 1, 0),
    (SOLVE, 0, 0),
    (ASSEMBLE, 0, 1),
    (RELAY, 1, 1, 0),
    (ASSEMBLE, 2, 0),
    (PASS, 0, 2, 0),
    (RELAY, 0, 1, 1),
    (SOLVE, 1, 0),
    (SOLVE, 0, 1),
    (PASS, 0, 2, 1),
    (ASSEMBLE, 3, 0),
    (PASS, 0, 3, 0),
    (SOLVE, 2, 0),
    (SOLVE, 1, 1),
    (PASS, 1, 3, 0),
    (PASS, 0, 3, 1),
    (SOLVE, 2, 1),
    (PASS, 1, 3, 1),
)
GATES = ((PLANE, 1, 0), (ASSEMBLE, 0, 0), (DOWN, 0, 0, 0), (DOWN, 0, 1, 0))
TIES = {
    (RELAY, 0, 1, 0): ((PLANE, 1, 0),),
    (RELAY, 1, 1, 0): ((PLANE, 2, 0),),
}
COSTS = {}


def params(mib):
    return pltpu.CompilerParams(vmem_limit_bytes=mib * MIB)


def cost(key):
    return pl.CostEstimate(flops=COSTS.get(key, 0), bytes_accessed=0, transcendentals=0)


def in_vmem():
    return pl.BlockSpec(memory_space=pltpu.VMEM)


def in_hbm():
    return pl.BlockSpec(memory_space=pltpu.HBM)


def after(values, earlier):
    values, earlier = tuple(values), tuple(earlier)
    return lax.optimization_barrier(values + earlier)[: len(values)]


def contract(left, right):
    return jnp.dot(left, right, preferred_element_type=jnp.float32)


def group_of(owner_ref, block, count):
    found = jnp.int32(0)
    for place in range(count):
        found = found + jnp.where(owner_ref[0, place] == block, place, 0)
    return found


def payload_kernel(pieces, count, owner_ref, rows_ref, factor_ref, index_ref, *refs):
    outs, (rows_held, factor_held, semaphores) = refs[:-3], refs[-3:]
    tiles, tile_rows, _ = rows_ref.shape
    chips = tiles // CORES
    capacity = factor_ref.shape[1] // count
    own = lax.axis_index("rhs")
    chip, core = lax.div(own, CORES), lax.rem(own, CORES)
    height = rows_held.shape[0] // tiles
    origin = pieces[0][1] * height if height < tile_rows else 0

    def window(block):
        return pl.ds(pl.multiple_of(group_of(owner_ref, block, count) * capacity, capacity), capacity)

    def tile(place):
        chip_tile = jnp.bitwise_xor(chip, place // CORES) * CORES
        return chip_tile + (core if place % CORES == 0 else (CORES - 1) - core)

    windows = [
        pltpu.make_async_copy(
            factor_ref.at[:, window(block)], factor_held.at[position], semaphores.at[position]
        )
        for position, (block, _, _) in enumerate(pieces)
    ]
    loads = [
        pltpu.make_async_copy(
            rows_ref.at[tile(place), pl.ds(origin, height)],
            rows_held.at[pl.ds(place * height, height)],
            semaphores.at[len(pieces) + place],
        )
        for place in range(tiles)
    ]
    for copy in [*windows[:1], *loads, *windows[1:]]:
        copy.start()
    if pieces[0][:2] == (0, 0):
        lists = [index_ref[:, window(block)] for block in range(count)]
        lists.append(jnp.full((INDEX_ROWS - count, capacity), -1, jnp.int32))
        table = jnp.concatenate(lists, axis=0).astype(jnp.float32)
        for out_ref in outs[:CORES]:
            for offset in range(chips):
                out_ref[offset, out_ref.shape[1] - INDEX_ROWS :, :] = table
    batch = min(BATCH, tiles)
    for position, (block, part, parts) in enumerate(pieces):
        windows[position].wait()
        wanted = tile_rows // parts
        for begin in range(0, tiles, batch):
            if position == 0:
                for place in range(begin, begin + batch):
                    loads[place].wait()
            product = contract(
                rows_held[begin * height : (begin + batch) * height], factor_held[position]
            )
            for place in range(begin, begin + batch):
                base = (place - begin) * height + part * wanted - origin
                outs[position * CORES + place % CORES][place // CORES, :wanted, :] = product[
                    base : base + wanted
                ]


def payload(pieces, mib, owner, rows, factor, index, count):
    tiles, tile_rows, depth = rows.shape
    chips = tiles // CORES
    capacity = factor.shape[1] // count
    height = tile_rows // pieces[0][2] if len(pieces) == 1 else tile_rows
    shapes = []
    for block, part, parts in pieces:
        extra = INDEX_ROWS if (block, part) == (0, 0) else 0
        shape = (chips, tile_rows // parts + extra, capacity)
        shapes += [jax.ShapeDtypeStruct(shape, jnp.float32)] * CORES
    outs = pl.pallas_call(
        functools.partial(payload_kernel, pieces, count),
        name="payload",
        out_shape=shapes,
        in_specs=[pl.BlockSpec(memory_space=pltpu.SMEM), in_hbm(), in_hbm(), in_vmem()],
        out_specs=[in_vmem()] * len(shapes),
        scratch_shapes=[
            pltpu.VMEM((tiles * height, depth), rows.dtype),
            pltpu.VMEM((len(pieces), depth, capacity), factor.dtype),
            pltpu.SemaphoreType.DMA((len(pieces) + tiles,)),
        ],
        compiler_params=params(mib),
        cost_estimate=cost((PAYLOAD,)),
    )(owner, rows, factor, index)
    return [outs[place : place + CORES] for place in range(0, len(outs), CORES)]


def assemble_kernel(block, block_size, height, chips, *refs):
    values_refs, index_refs, outs = refs[:chips], refs[chips : 2 * chips], refs[2 * chips :]
    capacity = values_refs[0].shape[2]
    index_row = index_refs[0].shape[1] - INDEX_ROWS + block
    places = lax.broadcasted_iota(jnp.int32, (block_size, capacity), 0)
    sources = [(chip, core) for chip in range(chips) for core in range(CORES)]
    total = None
    for first in range(0, len(sources), SOURCES):
        chosen = sources[first : first + SOURCES]
        values = jnp.concatenate(
            [values_refs[chip][core, :height, :] for chip, core in chosen], axis=1
        )
        spread = jnp.concatenate(
            [
                jnp.where(
                    places == index_refs[chip][core, pl.ds(index_row, 1), :].astype(jnp.int32),
                    1.0,
                    0.0,
                ).astype(jnp.bfloat16)
                for chip, core in chosen
            ],
            axis=1,
        )
        high = values.astype(jnp.bfloat16)
        low = (values - high.astype(jnp.float32)).astype(jnp.bfloat16)
        both = lax.dot_general(
            jnp.concatenate([high, low], axis=0),
            spread,
            (((1,), (1,)), ((), ())),
            preferred_element_type=jnp.float32,
        )
        both = both[:height] + both[height:]
        total = both if total is None else total + both
    part_rows = height // len(outs)
    for part, out_ref in enumerate(outs):
        out_ref[...] = total[part * part_rows : (part + 1) * part_rows]


def assemble(block, arrived, holders, height, parts, block_size):
    chips = len(arrived)
    capacity = arrived[0].shape[2]
    piece = jax.ShapeDtypeStruct((height // parts, block_size), jnp.float32)
    return pl.pallas_call(
        functools.partial(assemble_kernel, block, block_size, height, chips),
        name="assemble",
        out_shape=[piece] * parts,
        in_specs=[in_vmem()] * (2 * chips),
        out_specs=[in_vmem()] * parts,
        compiler_params=params(24),
        cost_estimate=cost((ASSEMBLE, block, 0)),
    )(*arrived, *holders)


def stage_kernel(factor_ref, inverse_ref, *refs):
    outs, semaphores = refs[:-1], refs[-1]
    width = inverse_ref.shape[1]
    sources = [inverse_ref] + [
        factor_ref.at[:, pl.ds(block * width, width)] for block in range(1, len(outs))
    ]
    copies = [
        pltpu.make_async_copy(source, out, semaphores.at[place])
        for place, (source, out) in enumerate(zip(sources, outs))
    ]
    for copy in copies:
        copy.start()
    for copy in copies:
        copy.wait()


def stage(factor, inverse, count):
    depth, width = inverse.shape
    piece = jax.ShapeDtypeStruct((depth, width), inverse.dtype)
    return pl.pallas_call(
        stage_kernel,
        name="stage",
        out_shape=[piece] * count,
        in_specs=[in_hbm()] * 2,
        out_specs=[in_vmem()] * count,
        scratch_shapes=[pltpu.SemaphoreType.DMA((count,))],
        compiler_params=params(16),
        cost_estimate=cost((STAGE,)),
    )(factor, inverse)


def pick(group, part):
    return list(group) if part is None or len(group) == 1 else [group[part]]


def rows_of(refs, part, rows):
    if part is None:
        return refs[0][...] if len(refs) == 1 else jnp.concatenate([ref[...] for ref in refs], axis=0)
    if refs[0].shape[0] == rows:
        return refs[0][...]
    return refs[0][pl.ds(part * rows, rows), :]


def split(refs, counts):
    groups, refs = [], list(refs)
    for count in counts:
        groups.append(refs[:count])
        refs = refs[count:]
    return groups, refs


def station_kernel(station, part, counts, terms, has_next, held, *refs):
    groups, refs = split(refs, counts)
    right, inverse, rest = groups[0], groups[1][0], groups[2:]
    rows = right[0].shape[0] // PARTS
    ready = rest[terms + held :] if held else []
    solved_ref = refs[0].at[pl.ds(part * rows, rows)] if ready else refs[0]
    place = lax.axis_index("col")

    @pl.when(place == station)
    def _():
        reduced = rows_of(right, part, rows)
        for group in rest[:terms]:
            reduced = reduced - rows_of(group, part, rows)
        solved = contract(reduced.astype(jnp.bfloat16), inverse[...])
        solved_ref[...] = solved
        if has_next:
            onward = contract(solved.astype(jnp.bfloat16), rest[terms][0][...])
            for group in rest[terms + 1 :]:
                onward = onward + rows_of(group, part, rows)
            refs[1][...] = onward

    for earlier in range(held):

        @pl.when(place == earlier)
        def _(earlier=earlier):
            solved_ref[...] = rest[terms + earlier][0][...]

    for done, group in enumerate(ready):
        refs[0][pl.ds(done * rows, rows), :] = group[0][...]


def station_step(station, part, right, inverse, terms, factor, extra, held, ready):
    rows, width = right.shape[0] // PARTS, right.shape[1]
    groups = [[right], [inverse], *terms, *([] if factor is None else [[factor]]), *extra, *held, *ready]
    operands = [array for group in groups for array in group]
    piece = jax.ShapeDtypeStruct((rows * (len(ready) + 1), width), jnp.float32)
    count = 1 if factor is None else 2
    return pl.pallas_call(
        functools.partial(
            station_kernel, station, part, [len(group) for group in groups], len(terms),
            factor is not None, len(held),
        ),
        name="solve",
        out_shape=[piece] * count,
        in_specs=[in_vmem()] * len(operands),
        out_specs=[in_vmem()] * count,
        compiler_params=params(16),
        cost_estimate=cost((SOLVE, station, part)),
    )(*operands)


def onward_kernel(station, part, counts, *refs):
    groups, refs = split(refs, counts)

    @pl.when(lax.axis_index("col") == station)
    def _():
        rows = refs[0].shape[0]
        onward = contract(rows_of(groups[0], None, rows).astype(jnp.bfloat16), groups[1][0][...])
        for group in groups[2:]:
            onward = onward + rows_of(group, part, rows)
        refs[0][...] = onward


def onward_step(station, part, solved, factor, extra, key):
    rows, width = sum(array.shape[0] for array in solved), solved[0].shape[1]
    groups = [solved, [factor], *extra]
    operands = [array for group in groups for array in group]
    return pl.pallas_call(
        functools.partial(onward_kernel, station, part, [len(group) for group in groups]),
        name="onward",
        out_shape=jax.ShapeDtypeStruct((rows, width), jnp.float32),
        in_specs=[in_vmem()] * len(operands),
        out_specs=in_vmem(),
        compiler_params=params(16),
        cost_estimate=cost(key),
    )(*operands)


def local(desc_rows, upd_factor, update_index, owner_map, sep_rhs, factor_rows, diag_inverse):
    count = lax.axis_size("col")
    tiles = lax.axis_size("rhs")
    chips = tiles // CORES
    block_size = diag_inverse.shape[0]
    tile_rows = sep_rhs.shape[0]
    flow_parts = [FLOW_PARTS[min(block, len(FLOW_PARTS) - 1)] for block in range(count)]

    results, transfers, token = {}, {}, []
    arrived, partial, flow, sums, held, relayed, weights = {}, {}, {}, {}, {}, {}, {}
    risen = {block: {} for block in range(count)}

    def ordered(key, values):
        wanted = [array for group in values for array in group]
        earlier = list(token)
        for tie in TIES.get(key, ()):
            earlier += transfers.get(tie, [])
        if earlier:
            wanted = list(after(wanted, earlier))
        return split(wanted, [len(group) for group in values])[0]

    def moved(value, pairs, key):
        received = lax.ppermute(value, "col", pairs)
        transfers[key] = [received]
        return received

    def both_cores(mine, other):
        received = lax.ppermute(other, "rhs", [(p, p ^ 1) for p in range(tiles)])
        return [jnp.stack([mine[offset], received[offset]]) for offset in range(chips)]

    def exchange(pieces, gate, key):
        gates = transfers.get(gate) or results.get(gate)
        received = []
        for offset in range(1, chips):
            value = pieces[offset]
            if gates:
                value = after([value], [gates[(offset - 1) % len(gates)]])[0]
            pairs = [(p, p ^ (offset * CORES)) for p in range(tiles)]
            received.append(lax.ppermute(value, "rhs", pairs))
        transfers[key] = received
        arrived[key] = [pieces[0], *received]

    rows = desc_rows[0].reshape(tiles, tile_rows, block_size)
    wanted = [(0, part, PARTS) for part in range(PARTS)]
    wanted += [(block, 0, 1) for block in range(1, count)]
    first = payload(
        tuple(wanted[:1]), FIRST_MIB, owner_map, rows, upd_factor[0], update_index, count
    )
    payloads = [both_cores(*first[0])]
    token += [payloads[0][0]]

    hops = {0: []}
    stride = 1
    while stride < count:
        hops[0].append([(p + stride, p) for p in range(0, count - stride, 2 * stride)])
        stride *= 2
    for block in range(1, count):
        hops[block] = [[(p, p - 1)] for p in range(count - 1, block, -1)]

    def rest():
        late = ordered((PAYLOAD,), [[rows]])[0][0]
        pairs = payload(
            tuple(wanted[1:]), REST_MIB, owner_map, late, upd_factor[0], update_index, count
        )
        results[PAYLOAD] = pairs
        return pairs[0][:1]

    def load():
        groups = ordered((STAGE,), [[factor_rows], [diag_inverse]])
        got = stage(groups[0][0], groups[1][0], count)
        weights.update(enumerate(got))
        return got[:1]

    def send_block(block):
        gate = GATES[min(block, len(GATES) - 1)]
        exchange(payloads[PARTS + block - 1], gate, (PLANE, block, 0))

    def start_flow(block, part):
        flow[block, part] = [partial[block][part]]
        if hops[block]:
            flow[block, part].append(
                moved(partial[block][part], hops[block][0], (DOWN, block, 0, part))
            )

    def assemble_part(part):
        key = (ASSEMBLE, 0, part)
        values = ordered(key, [arrived[PLANE, 0, part], arrived[PLANE, 0, 0]])
        done = assemble(
            0, values[0], values[1], tile_rows // PARTS, flow_parts[0] // PARTS, block_size
        )
        results[key] = done
        if part == 0:
            for mine, other in results[PAYLOAD]:
                payloads.append(both_cores(mine, after([other], done[:1])[0]))
            send_block(1)
        if part + 1 < PARTS:
            exchange(payloads[part + 1], GATES[0], (PLANE, 0, part + 1))
        partial.setdefault(0, []).extend(done)
        for place in range(part * len(done), (part + 1) * len(done)):
            start_flow(0, place)
        return done

    def assemble_block(block):
        key = (ASSEMBLE, block, 0)
        values = ordered(key, [arrived[PLANE, block, 0], arrived[PLANE, 0, 0]])
        done = assemble(block, values[0], values[1], tile_rows, flow_parts[block], block_size)
        results[key] = partial[block] = done
        if block + 1 < count:
            send_block(block + 1)
        for part in range(flow_parts[block]):
            start_flow(block, part)
        return done

    def relay(block, hop, part):
        terms = flow[block, part]
        base = sums.get((block, part), terms[0])
        groups = ordered((RELAY, block, hop, part), [[base], [terms[-1]]])
        value = groups[0][0] + groups[1][0]
        received = moved(value, hops[block][hop], (DOWN, block, hop, part))
        if block == 0:
            flow[block, part] = [*terms, received]
            sums[block, part] = value
        else:
            flow[block, part] = [terms[0], received]
        return [value]

    def solve(station, part):
        last = station + 1 == count
        key = (SOLVE, station, part)
        terms = [[array] for array in flow[station, part if flow_parts[station] > 1 else 0]]
        terms += [[array] for array in risen[station].get(part, [])]
        extra = [] if last else [pick(partial[station + 1], part)]
        groups = ordered(key, [*terms, *extra])
        outs = station_step(
            station, part, sep_rhs, weights[0], groups[: len(terms)],
            None if last else weights[station + 1], groups[len(terms) :],
            [[held[part, k]] for k in range(station)] if last else [],
            [[held[p, station]] for p in range(part)] if last and part + 1 == PARTS else [],
        )
        held[part, station] = outs[0]
        if not last:
            received = moved(
                outs[1], [(station, station + 1)], (UP, station, station + 1, part)
            )
            risen[station + 1].setdefault(part, []).append(received)
        return outs[:1]

    def pass_on(station, block, part):
        key = (PASS, station, block, part)
        onto = block if station + 2 == block else station + 1
        extra = [pick(partial[block], part)]
        if (block, part) in relayed:
            extra.append([relayed.pop((block, part))])
        groups = ordered(key, [[held[part, station]], *extra])
        value = onward_step(station, part, groups[0], weights[block], groups[1:], key)
        received = moved(value, [(station, onto)], (UP, station, block, part))
        if onto == block:
            risen[block].setdefault(part, []).append(received)
        else:
            relayed[block, part] = received
        return [value]

    events = {(PAYLOAD,): rest, (STAGE,): load}
    requires = {}
    for part in range(PARTS):
        events[ASSEMBLE, 0, part] = functools.partial(assemble_part, part)
        requires[ASSEMBLE, 0, part] = [(ASSEMBLE, 0, p) for p in range(part)]
    for block in range(count):
        below = [(ASSEMBLE, b, 0) for b in range(1, min(block + 2, count))]
        if block:
            events[ASSEMBLE, block, 0] = functools.partial(assemble_block, block)
            requires[ASSEMBLE, block, 0] = below[: block - 1]
        for part in range(flow_parts[block]):
            own = below[:block] or [(ASSEMBLE, 0, part * PARTS // flow_parts[0])]
            for hop in range(1, len(hops[block])):
                events[RELAY, block, hop, part] = functools.partial(relay, block, hop, part)
                requires[RELAY, block, hop, part] = own + [
                    (RELAY, block, h, part) for h in range(1, hop)
                ]
        for part in range(PARTS):
            events[SOLVE, block, part] = functools.partial(solve, block, part)
            flowing = part if flow_parts[block] > 1 else 0
            requires[SOLVE, block, part] = [
                *below,
                *([] if block else [(ASSEMBLE, 0, p) for p in range(part + 1)]),
                *[(RELAY, block, hop, flowing) for hop in range(1, len(hops[block]))],
                *[(SOLVE, k, p) for k in range(block) for p in range(part + 1)],
                *[(SOLVE, block, p) for p in range(part)],
                *[(PASS, k, block, part) for k in range(block - 1)],
            ]
            for k in range(block - 1):
                events[PASS, k, block, part] = functools.partial(pass_on, k, block, part)
                requires[PASS, k, block, part] = [
                    *below[:block],
                    *[(SOLVE, k, p) for p in range(part + 1)],
                    *[(PASS, e, block, part) for e in range(k)],
                ]

    def run(key):
        if key in token_of or key not in events:
            return
        for earlier in requires.get(key, ()):
            run(earlier)
        token_of[key] = events[key]()
        token[:] = token_of[key][:1]

    token_of = {}
    exchange(payloads[0], None, (PLANE, 0, 0))
    for key in ((PAYLOAD,), (ASSEMBLE, 0, 0), (STAGE,), *ORDER):
        run(key)
    for part in range(PARTS):
        run((SOLVE, count - 1, part))
    return held[PARTS - 1, count - 1]


def solution(mesh):
    placed = (
        P(("col", "rhs"), None, None),
        P(("col", "rhs"), None, None),
        P(("col", "rhs"), None),
        P(("col", "rhs"), None),
        P("rhs", "col"),
        P("col", None),
        P("col", None),
    )
    return jax.shard_map(
        local, mesh=mesh, in_specs=placed, out_specs=P("rhs", "col"), check_vma=False
    )
```

```python
import functools

import jax
import jax.numpy as jnp
from jax import lax
from jax.experimental import pallas as pl
from jax.experimental.pallas import tpu as pltpu
from jax.sharding import PartitionSpec as P

MIB = 1024 * 1024
STAGE, PAYLOAD, ASSEMBLE, RELAY, SOLVE, PASS, PLANE, DOWN, UP = range(9)
CORES = 2
INDEX_ROWS = 8
SOURCES = 4
PARTS = 2
BATCH = 4
FIRST_MIB, REST_MIB = 52, 40
FLOW_PARTS = (2, 1, 1, 1)
ORDER = (
    (RELAY, 0, 1, 0),
    (STAGE,),
    (ASSEMBLE, 1, 0),
    (ASSEMBLE, 0, 1),
    (SOLVE, 0, 0),
    (RELAY, 1, 1, 0),
    (ASSEMBLE, 2, 0),
    (PASS, 0, 2, 0),
    (RELAY, 0, 1, 1),
    (SOLVE, 1, 0),
    (PASS, 0, 2, 1),
    (ASSEMBLE, 3, 0),
    (SOLVE, 0, 1),
    (PASS, 0, 3, 0),
    (SOLVE, 2, 0),
    (SOLVE, 1, 1),
    (PASS, 1, 3, 0),
    (PASS, 0, 3, 1),
    (SOLVE, 2, 1),
    (PASS, 1, 3, 1),
)
GATES = ((PLANE, 1, 0), (ASSEMBLE, 0, 0), (DOWN, 0, 0, 0), (DOWN, 0, 1, 0))
TIES = {
    (RELAY, 0, 1, 0): ((PLANE, 1, 0),),
    (RELAY, 1, 1, 0): ((PLANE, 2, 0),),
}
COSTS = {}


def params(mib):
    return pltpu.CompilerParams(vmem_limit_bytes=mib * MIB)


def cost(key):
    return pl.CostEstimate(flops=COSTS.get(key, 0), bytes_accessed=0, transcendentals=0)


def in_vmem():
    return pl.BlockSpec(memory_space=pltpu.VMEM)


def in_hbm():
    return pl.BlockSpec(memory_space=pltpu.HBM)


def after(values, earlier):
    values, earlier = tuple(values), tuple(earlier)
    return lax.optimization_barrier(values + earlier)[: len(values)]


def contract(left, right):
    return jnp.dot(left, right, preferred_element_type=jnp.float32)


def group_of(owner_ref, block, count):
    found = jnp.int32(0)
    for place in range(count):
        found = found + jnp.where(owner_ref[0, place] == block, place, 0)
    return found


def payload_kernel(pieces, count, owner_ref, rows_ref, factor_ref, index_ref, *refs):
    outs, (rows_held, factor_held, semaphores) = refs[:-3], refs[-3:]
    tiles, tile_rows, _ = rows_ref.shape
    chips = tiles // CORES
    capacity = factor_ref.shape[1] // count
    own = lax.axis_index("rhs")
    chip, core = lax.div(own, CORES), lax.rem(own, CORES)
    height = rows_held.shape[0] // tiles
    origin = pieces[0][1] * height if height < tile_rows else 0

    def window(block):
        return pl.ds(pl.multiple_of(group_of(owner_ref, block, count) * capacity, capacity), capacity)

    def tile(place):
        chip_tile = jnp.bitwise_xor(chip, place // CORES) * CORES
        return chip_tile + (core if place % CORES == 0 else (CORES - 1) - core)

    windows = [
        pltpu.make_async_copy(
            factor_ref.at[:, window(block)], factor_held.at[position], semaphores.at[position]
        )
        for position, (block, _, _) in enumerate(pieces)
    ]
    loads = [
        pltpu.make_async_copy(
            rows_ref.at[tile(place), pl.ds(origin, height)],
            rows_held.at[pl.ds(place * height, height)],
            semaphores.at[len(pieces) + place],
        )
        for place in range(tiles)
    ]
    for copy in [*windows[:1], *loads, *windows[1:]]:
        copy.start()
    if pieces[0][:2] == (0, 0):
        lists = [index_ref[:, window(block)] for block in range(count)]
        lists.append(jnp.full((INDEX_ROWS - count, capacity), -1, jnp.int32))
        table = jnp.concatenate(lists, axis=0).astype(jnp.float32)
        for out_ref in outs[:CORES]:
            for offset in range(chips):
                out_ref[offset, out_ref.shape[1] - INDEX_ROWS :, :] = table
    batch = min(BATCH, tiles)
    for position, (block, part, parts) in enumerate(pieces):
        windows[position].wait()
        wanted = tile_rows // parts
        for begin in range(0, tiles, batch):
            if position == 0:
                for place in range(begin, begin + batch):
                    loads[place].wait()
            product = contract(
                rows_held[begin * height : (begin + batch) * height], factor_held[position]
            )
            for place in range(begin, begin + batch):
                base = (place - begin) * height + part * wanted - origin
                outs[position * CORES + place % CORES][place // CORES, :wanted, :] = product[
                    base : base + wanted
                ]


def payload(pieces, mib, owner, rows, factor, index, count):
    tiles, tile_rows, depth = rows.shape
    chips = tiles // CORES
    capacity = factor.shape[1] // count
    height = tile_rows // pieces[0][2] if len(pieces) == 1 else tile_rows
    shapes = []
    for block, part, parts in pieces:
        extra = INDEX_ROWS if (block, part) == (0, 0) else 0
        shape = (chips, tile_rows // parts + extra, capacity)
        shapes += [jax.ShapeDtypeStruct(shape, jnp.float32)] * CORES
    outs = pl.pallas_call(
        functools.partial(payload_kernel, pieces, count),
        name="payload",
        out_shape=shapes,
        in_specs=[pl.BlockSpec(memory_space=pltpu.SMEM), in_hbm(), in_hbm(), in_vmem()],
        out_specs=[in_vmem()] * len(shapes),
        scratch_shapes=[
            pltpu.VMEM((tiles * height, depth), rows.dtype),
            pltpu.VMEM((len(pieces), depth, capacity), factor.dtype),
            pltpu.SemaphoreType.DMA((len(pieces) + tiles,)),
        ],
        compiler_params=params(mib),
        cost_estimate=cost((PAYLOAD,)),
    )(owner, rows, factor, index)
    return [outs[place : place + CORES] for place in range(0, len(outs), CORES)]


def assemble_kernel(block, block_size, height, chips, *refs):
    values_refs, index_refs, outs = refs[:chips], refs[chips : 2 * chips], refs[2 * chips :]
    capacity = values_refs[0].shape[2]
    index_row = index_refs[0].shape[1] - INDEX_ROWS + block
    places = lax.broadcasted_iota(jnp.int32, (block_size, capacity), 0)
    sources = [(chip, core) for chip in range(chips) for core in range(CORES)]
    total = None
    for first in range(0, len(sources), SOURCES):
        chosen = sources[first : first + SOURCES]
        values = jnp.concatenate(
            [values_refs[chip][core, :height, :] for chip, core in chosen], axis=1
        )
        spread = jnp.concatenate(
            [
                jnp.where(
                    places == index_refs[chip][core, pl.ds(index_row, 1), :].astype(jnp.int32),
                    1.0,
                    0.0,
                ).astype(jnp.bfloat16)
                for chip, core in chosen
            ],
            axis=1,
        )
        high = values.astype(jnp.bfloat16)
        low = (values - high.astype(jnp.float32)).astype(jnp.bfloat16)
        both = lax.dot_general(
            jnp.concatenate([high, low], axis=0),
            spread,
            (((1,), (1,)), ((), ())),
            preferred_element_type=jnp.float32,
        )
        both = both[:height] + both[height:]
        total = both if total is None else total + both
    part_rows = height // len(outs)
    for part, out_ref in enumerate(outs):
        out_ref[...] = total[part * part_rows : (part + 1) * part_rows]


def assemble(block, arrived, holders, height, parts, block_size):
    chips = len(arrived)
    capacity = arrived[0].shape[2]
    piece = jax.ShapeDtypeStruct((height // parts, block_size), jnp.float32)
    return pl.pallas_call(
        functools.partial(assemble_kernel, block, block_size, height, chips),
        name="assemble",
        out_shape=[piece] * parts,
        in_specs=[in_vmem()] * (2 * chips),
        out_specs=[in_vmem()] * parts,
        compiler_params=params(24),
        cost_estimate=cost((ASSEMBLE, block, 0)),
    )(*arrived, *holders)


def stage_kernel(factor_ref, inverse_ref, *refs):
    outs, semaphores = refs[:-1], refs[-1]
    width = inverse_ref.shape[1]
    sources = [inverse_ref] + [
        factor_ref.at[:, pl.ds(block * width, width)] for block in range(1, len(outs))
    ]
    copies = [
        pltpu.make_async_copy(source, out, semaphores.at[place])
        for place, (source, out) in enumerate(zip(sources, outs))
    ]
    for copy in copies:
        copy.start()
    for copy in copies:
        copy.wait()


def stage(factor, inverse, count):
    depth, width = inverse.shape
    piece = jax.ShapeDtypeStruct((depth, width), inverse.dtype)
    return pl.pallas_call(
        stage_kernel,
        name="stage",
        out_shape=[piece] * count,
        in_specs=[in_hbm()] * 2,
        out_specs=[in_vmem()] * count,
        scratch_shapes=[pltpu.SemaphoreType.DMA((count,))],
        compiler_params=params(16),
        cost_estimate=cost((STAGE,)),
    )(factor, inverse)


def pick(group, part):
    return list(group) if part is None or len(group) == 1 else [group[part]]


def rows_of(refs, part, rows):
    if part is None:
        return refs[0][...] if len(refs) == 1 else jnp.concatenate([ref[...] for ref in refs], axis=0)
    if refs[0].shape[0] == rows:
        return refs[0][...]
    return refs[0][pl.ds(part * rows, rows), :]


def split(refs, counts):
    groups, refs = [], list(refs)
    for count in counts:
        groups.append(refs[:count])
        refs = refs[count:]
    return groups, refs


def station_kernel(station, part, counts, terms, has_next, held, *refs):
    groups, refs = split(refs, counts)
    right, inverse, rest = groups[0], groups[1][0], groups[2:]
    rows = right[0].shape[0] // PARTS
    ready = rest[terms + held :] if held else []
    solved_ref = refs[0].at[pl.ds(part * rows, rows)] if ready else refs[0]
    place = lax.axis_index("col")

    @pl.when(place == station)
    def _():
        reduced = rows_of(right, part, rows)
        for group in rest[:terms]:
            reduced = reduced - rows_of(group, part, rows)
        solved = contract(reduced.astype(jnp.bfloat16), inverse[...])
        solved_ref[...] = solved
        if has_next:
            onward = contract(solved.astype(jnp.bfloat16), rest[terms][0][...])
            for group in rest[terms + 1 :]:
                onward = onward + rows_of(group, part, rows)
            refs[1][...] = onward

    for earlier in range(held):

        @pl.when(place == earlier)
        def _(earlier=earlier):
            solved_ref[...] = rest[terms + earlier][0][...]

    for done, group in enumerate(ready):
        refs[0][pl.ds(done * rows, rows), :] = group[0][...]


def station_step(station, part, right, inverse, terms, factor, extra, held, ready):
    rows, width = right.shape[0] // PARTS, right.shape[1]
    groups = [[right], [inverse], *terms, *([] if factor is None else [[factor]]), *extra, *held, *ready]
    operands = [array for group in groups for array in group]
    piece = jax.ShapeDtypeStruct((rows * (len(ready) + 1), width), jnp.float32)
    count = 1 if factor is None else 2
    return pl.pallas_call(
        functools.partial(
            station_kernel, station, part, [len(group) for group in groups], len(terms),
            factor is not None, len(held),
        ),
        name="solve",
        out_shape=[piece] * count,
        in_specs=[in_vmem()] * len(operands),
        out_specs=[in_vmem()] * count,
        compiler_params=params(16),
        cost_estimate=cost((SOLVE, station, part)),
    )(*operands)


def onward_kernel(station, part, counts, *refs):
    groups, refs = split(refs, counts)

    @pl.when(lax.axis_index("col") == station)
    def _():
        rows = refs[0].shape[0]
        onward = contract(rows_of(groups[0], None, rows).astype(jnp.bfloat16), groups[1][0][...])
        for group in groups[2:]:
            onward = onward + rows_of(group, part, rows)
        refs[0][...] = onward


def onward_step(station, part, solved, factor, extra, key):
    rows, width = sum(array.shape[0] for array in solved), solved[0].shape[1]
    groups = [solved, [factor], *extra]
    operands = [array for group in groups for array in group]
    return pl.pallas_call(
        functools.partial(onward_kernel, station, part, [len(group) for group in groups]),
        name="onward",
        out_shape=jax.ShapeDtypeStruct((rows, width), jnp.float32),
        in_specs=[in_vmem()] * len(operands),
        out_specs=in_vmem(),
        compiler_params=params(16),
        cost_estimate=cost(key),
    )(*operands)


def local(desc_rows, upd_factor, update_index, owner_map, sep_rhs, factor_rows, diag_inverse):
    count = lax.axis_size("col")
    tiles = lax.axis_size("rhs")
    chips = tiles // CORES
    block_size = diag_inverse.shape[0]
    tile_rows = sep_rhs.shape[0]
    flow_parts = [FLOW_PARTS[min(block, len(FLOW_PARTS) - 1)] for block in range(count)]

    results, transfers, token = {}, {}, []
    arrived, partial, flow, sums, held, relayed, weights = {}, {}, {}, {}, {}, {}, {}
    risen = {block: {} for block in range(count)}

    def ordered(key, values):
        wanted = [array for group in values for array in group]
        earlier = list(token)
        for tie in TIES.get(key, ()):
            earlier += transfers.get(tie, [])
        if earlier:
            wanted = list(after(wanted, earlier))
        return split(wanted, [len(group) for group in values])[0]

    def moved(value, pairs, key):
        received = lax.ppermute(value, "col", pairs)
        transfers[key] = [received]
        return received

    def both_cores(mine, other):
        received = lax.ppermute(other, "rhs", [(p, p ^ 1) for p in range(tiles)])
        return [jnp.stack([mine[offset], received[offset]]) for offset in range(chips)]

    def exchange(pieces, gate, key):
        gates = transfers.get(gate) or results.get(gate)
        received = []
        for offset in range(1, chips):
            value = pieces[offset]
            if gates:
                value = after([value], [gates[(offset - 1) % len(gates)]])[0]
            pairs = [(p, p ^ (offset * CORES)) for p in range(tiles)]
            received.append(lax.ppermute(value, "rhs", pairs))
        transfers[key] = received
        arrived[key] = [pieces[0], *received]

    rows = desc_rows[0].reshape(tiles, tile_rows, block_size)
    wanted = [(0, part, PARTS) for part in range(PARTS)]
    wanted += [(block, 0, 1) for block in range(1, count)]
    first = payload(
        tuple(wanted[:1]), FIRST_MIB, owner_map, rows, upd_factor[0], update_index, count
    )
    payloads = [both_cores(*first[0])]
    token += [payloads[0][0]]

    hops = {0: []}
    stride = 1
    while stride < count:
        hops[0].append([(p + stride, p) for p in range(0, count - stride, 2 * stride)])
        stride *= 2
    for block in range(1, count):
        hops[block] = [[(p, p - 1)] for p in range(count - 1, block, -1)]

    def rest():
        late = ordered((PAYLOAD,), [[rows]])[0][0]
        pairs = payload(
            tuple(wanted[1:]), REST_MIB, owner_map, late, upd_factor[0], update_index, count
        )
        results[PAYLOAD] = pairs
        return pairs[0][:1]

    def load():
        groups = ordered((STAGE,), [[factor_rows], [diag_inverse]])
        got = stage(groups[0][0], groups[1][0], count)
        weights.update(enumerate(got))
        return got[:1]

    def send_block(block):
        gate = GATES[min(block, len(GATES) - 1)]
        exchange(payloads[PARTS + block - 1], gate, (PLANE, block, 0))

    def start_flow(block, part):
        flow[block, part] = [partial[block][part]]
        if hops[block]:
            flow[block, part].append(
                moved(partial[block][part], hops[block][0], (DOWN, block, 0, part))
            )

    def assemble_part(part):
        key = (ASSEMBLE, 0, part)
        values = ordered(key, [arrived[PLANE, 0, part], arrived[PLANE, 0, 0]])
        done = assemble(
            0, values[0], values[1], tile_rows // PARTS, flow_parts[0] // PARTS, block_size
        )
        results[key] = done
        if part == 0:
            for mine, other in results[PAYLOAD]:
                payloads.append(both_cores(mine, after([other], done[:1])[0]))
            send_block(1)
        if part + 1 < PARTS:
            exchange(payloads[part + 1], GATES[0], (PLANE, 0, part + 1))
        partial.setdefault(0, []).extend(done)
        for place in range(part * len(done), (part + 1) * len(done)):
            start_flow(0, place)
        return done

    def assemble_block(block):
        key = (ASSEMBLE, block, 0)
        values = ordered(key, [arrived[PLANE, block, 0], arrived[PLANE, 0, 0]])
        done = assemble(block, values[0], values[1], tile_rows, flow_parts[block], block_size)
        results[key] = partial[block] = done
        if block + 1 < count:
            send_block(block + 1)
        for part in range(flow_parts[block]):
            start_flow(block, part)
        return done

    def relay(block, hop, part):
        terms = flow[block, part]
        base = sums.get((block, part), terms[0])
        groups = ordered((RELAY, block, hop, part), [[base], [terms[-1]]])
        value = groups[0][0] + groups[1][0]
        received = moved(value, hops[block][hop], (DOWN, block, hop, part))
        if block == 0:
            flow[block, part] = [*terms, received]
            sums[block, part] = value
        else:
            flow[block, part] = [terms[0], received]
        return [value]

    def solve(station, part):
        last = station + 1 == count
        key = (SOLVE, station, part)
        terms = [[array] for array in flow[station, part if flow_parts[station] > 1 else 0]]
        terms += [[array] for array in risen[station].get(part, [])]
        extra = [] if last else [pick(partial[station + 1], part)]
        groups = ordered(key, [*terms, *extra])
        outs = station_step(
            station, part, sep_rhs, weights[0], groups[: len(terms)],
            None if last else weights[station + 1], groups[len(terms) :],
            [[held[part, k]] for k in range(station)] if last else [],
            [[held[p, station]] for p in range(part)] if last and part + 1 == PARTS else [],
        )
        held[part, station] = outs[0]
        if not last:
            received = moved(
                outs[1], [(station, station + 1)], (UP, station, station + 1, part)
            )
            risen[station + 1].setdefault(part, []).append(received)
        return outs[:1]

    def pass_on(station, block, part):
        key = (PASS, station, block, part)
        onto = block if station + 2 == block else station + 1
        extra = [pick(partial[block], part)]
        if (block, part) in relayed:
            extra.append([relayed.pop((block, part))])
        groups = ordered(key, [[held[part, station]], *extra])
        value = onward_step(station, part, groups[0], weights[block], groups[1:], key)
        received = moved(value, [(station, onto)], (UP, station, block, part))
        if onto == block:
            risen[block].setdefault(part, []).append(received)
        else:
            relayed[block, part] = received
        return [value]

    events = {(PAYLOAD,): rest, (STAGE,): load}
    requires = {}
    for part in range(PARTS):
        events[ASSEMBLE, 0, part] = functools.partial(assemble_part, part)
        requires[ASSEMBLE, 0, part] = [(ASSEMBLE, 0, p) for p in range(part)]
    for block in range(count):
        below = [(ASSEMBLE, b, 0) for b in range(1, min(block + 2, count))]
        if block:
            events[ASSEMBLE, block, 0] = functools.partial(assemble_block, block)
            requires[ASSEMBLE, block, 0] = below[: block - 1]
        for part in range(flow_parts[block]):
            own = below[:block] or [(ASSEMBLE, 0, part * PARTS // flow_parts[0])]
            for hop in range(1, len(hops[block])):
                events[RELAY, block, hop, part] = functools.partial(relay, block, hop, part)
                requires[RELAY, block, hop, part] = own + [
                    (RELAY, block, h, part) for h in range(1, hop)
                ]
        for part in range(PARTS):
            events[SOLVE, block, part] = functools.partial(solve, block, part)
            flowing = part if flow_parts[block] > 1 else 0
            requires[SOLVE, block, part] = [
                (STAGE,),
                *below,
                *([] if block else [(ASSEMBLE, 0, p) for p in range(part + 1)]),
                *[(RELAY, block, hop, flowing) for hop in range(1, len(hops[block]))],
                *[(SOLVE, k, p) for k in range(block) for p in range(part + 1)],
                *[(SOLVE, block, p) for p in range(part)],
                *[(PASS, k, block, part) for k in range(block - 1)],
            ]
            for k in range(block - 1):
                events[PASS, k, block, part] = functools.partial(pass_on, k, block, part)
                requires[PASS, k, block, part] = [
                    *below[:block],
                    *[(SOLVE, k, p) for p in range(part + 1)],
                    *[(PASS, e, block, part) for e in range(k)],
                ]

    def run(key):
        if key in token_of or key not in events:
            return
        for earlier in requires.get(key, ()):
            run(earlier)
        token_of[key] = events[key]()
        token[:] = token_of[key][:1]

    token_of = {}
    exchange(payloads[0], None, (PLANE, 0, 0))
    for key in ((PAYLOAD,), (ASSEMBLE, 0, 0), *ORDER):
        run(key)
    for part in range(PARTS):
        run((SOLVE, count - 1, part))
    return held[PARTS - 1, count - 1]


def solution(mesh):
    placed = (
        P(("col", "rhs"), None, None),
        P(("col", "rhs"), None, None),
        P(("col", "rhs"), None),
        P(("col", "rhs"), None),
        P("rhs", "col"),
        P("col", None),
        P("col", None),
    )
    return jax.shard_map(
        local, mesh=mesh, in_specs=placed, out_specs=P("rhs", "col"), check_vma=False
    )
```

```python
import functools

import jax
import jax.numpy as jnp
from jax import lax
from jax.experimental import pallas as pl
from jax.experimental.pallas import tpu as pltpu
from jax.sharding import PartitionSpec as P

MIB = 1024 * 1024
STAGE, PAYLOAD, ASSEMBLE, RELAY, SOLVE, PASS, PLANE, DOWN, UP = range(9)
CORES = 2
INDEX_ROWS = 8
SOURCES = 4
PARTS = 2
BATCH = 4
FIRST_MIB, REST_MIB = 52, 40
FLOW_PARTS = (2, 1, 1, 1)
ORDER = (
    (RELAY, 0, 1, 0),
    (STAGE,),
    (ASSEMBLE, 1, 0),
    (ASSEMBLE, 0, 1),
    (SOLVE, 0, 0),
    (RELAY, 1, 1, 0),
    (ASSEMBLE, 2, 0),
    (PASS, 0, 2, 0),
    (RELAY, 0, 1, 1),
    (SOLVE, 1, 0),
    (PASS, 0, 2, 1),
    (SOLVE, 2, 0),
    (ASSEMBLE, 3, 0),
    (SOLVE, 0, 1),
    (PASS, 0, 3, 0),
    (SOLVE, 1, 1),
    (PASS, 1, 3, 0),
    (PASS, 0, 3, 1),
    (SOLVE, 2, 1),
    (PASS, 1, 3, 1),
)
GATES = ((ASSEMBLE, 0, 0), (PLANE, 0, 0), (DOWN, 0, 0, 0), (DOWN, 0, 1, 0))
TIES = {
    (RELAY, 0, 1, 0): ((PLANE, 1, 0),),
}
COSTS = {(PAYLOAD,): 2000000000}


def params(mib):
    return pltpu.CompilerParams(vmem_limit_bytes=mib * MIB)


def cost(key):
    return pl.CostEstimate(flops=COSTS.get(key, 0), bytes_accessed=0, transcendentals=0)


def in_vmem():
    return pl.BlockSpec(memory_space=pltpu.VMEM)


def in_hbm():
    return pl.BlockSpec(memory_space=pltpu.HBM)


def after(values, earlier):
    values, earlier = tuple(values), tuple(earlier)
    return lax.optimization_barrier(values + earlier)[: len(values)]


def contract(left, right):
    return jnp.dot(left, right, preferred_element_type=jnp.float32)


def group_of(owner_ref, block, count):
    found = jnp.int32(0)
    for place in range(count):
        found = found + jnp.where(owner_ref[0, place] == block, place, 0)
    return found


def payload_kernel(pieces, count, owner_ref, rows_ref, factor_ref, index_ref, *refs):
    outs, (rows_held, factor_held, semaphores) = refs[:-3], refs[-3:]
    tiles, tile_rows, _ = rows_ref.shape
    chips = tiles // CORES
    capacity = factor_ref.shape[1] // count
    own = lax.axis_index("rhs")
    chip, core = lax.div(own, CORES), lax.rem(own, CORES)
    height = rows_held.shape[0] // tiles
    origin = pieces[0][1] * height if height < tile_rows else 0

    def window(block):
        return pl.ds(pl.multiple_of(group_of(owner_ref, block, count) * capacity, capacity), capacity)

    def tile(place):
        chip_tile = jnp.bitwise_xor(chip, place // CORES) * CORES
        return chip_tile + (core if place % CORES == 0 else (CORES - 1) - core)

    windows = [
        pltpu.make_async_copy(
            factor_ref.at[:, window(block)], factor_held.at[position], semaphores.at[position]
        )
        for position, (block, _, _) in enumerate(pieces)
    ]
    loads = [
        pltpu.make_async_copy(
            rows_ref.at[tile(place), pl.ds(origin, height)],
            rows_held.at[pl.ds(place * height, height)],
            semaphores.at[len(pieces) + place],
        )
        for place in range(tiles)
    ]
    for copy in [*windows[:1], *loads, *windows[1:]]:
        copy.start()
    if pieces[0][:2] == (0, 0):
        lists = [index_ref[:, window(block)] for block in range(count)]
        lists.append(jnp.full((INDEX_ROWS - count, capacity), -1, jnp.int32))
        table = jnp.concatenate(lists, axis=0).astype(jnp.float32)
        for out_ref in outs[:CORES]:
            for offset in range(chips):
                out_ref[offset, out_ref.shape[1] - INDEX_ROWS :, :] = table
    batch = min(BATCH, tiles)
    for position, (block, part, parts) in enumerate(pieces):
        windows[position].wait()
        wanted = tile_rows // parts
        for begin in range(0, tiles, batch):
            if position == 0:
                for place in range(begin, begin + batch):
                    loads[place].wait()
            product = contract(
                rows_held[begin * height : (begin + batch) * height], factor_held[position]
            )
            for place in range(begin, begin + batch):
                base = (place - begin) * height + part * wanted - origin
                outs[position * CORES + place % CORES][place // CORES, :wanted, :] = product[
                    base : base + wanted
                ]


def payload(pieces, mib, owner, rows, factor, index, count):
    tiles, tile_rows, depth = rows.shape
    chips = tiles // CORES
    capacity = factor.shape[1] // count
    height = tile_rows // pieces[0][2] if len(pieces) == 1 else tile_rows
    shapes = []
    for block, part, parts in pieces:
        extra = INDEX_ROWS if (block, part) == (0, 0) else 0
        shape = (chips, tile_rows // parts + extra, capacity)
        shapes += [jax.ShapeDtypeStruct(shape, jnp.float32)] * CORES
    outs = pl.pallas_call(
        functools.partial(payload_kernel, pieces, count),
        name="payload",
        out_shape=shapes,
        in_specs=[pl.BlockSpec(memory_space=pltpu.SMEM), in_hbm(), in_hbm(), in_vmem()],
        out_specs=[in_vmem()] * len(shapes),
        scratch_shapes=[
            pltpu.VMEM((tiles * height, depth), rows.dtype),
            pltpu.VMEM((len(pieces), depth, capacity), factor.dtype),
            pltpu.SemaphoreType.DMA((len(pieces) + tiles,)),
        ],
        compiler_params=params(mib),
        cost_estimate=cost((PAYLOAD,)),
    )(owner, rows, factor, index)
    return [outs[place : place + CORES] for place in range(0, len(outs), CORES)]


def assemble_kernel(block, block_size, height, chips, *refs):
    values_refs, index_refs, outs = refs[:chips], refs[chips : 2 * chips], refs[2 * chips :]
    capacity = values_refs[0].shape[2]
    index_row = index_refs[0].shape[1] - INDEX_ROWS + block
    places = lax.broadcasted_iota(jnp.int32, (block_size, capacity), 0)
    sources = [(chip, core) for chip in range(chips) for core in range(CORES)]
    total = None
    for first in range(0, len(sources), SOURCES):
        chosen = sources[first : first + SOURCES]
        values = jnp.concatenate(
            [values_refs[chip][core, :height, :] for chip, core in chosen], axis=1
        )
        spread = jnp.concatenate(
            [
                jnp.where(
                    places == index_refs[chip][core, pl.ds(index_row, 1), :].astype(jnp.int32),
                    1.0,
                    0.0,
                ).astype(jnp.bfloat16)
                for chip, core in chosen
            ],
            axis=1,
        )
        high = values.astype(jnp.bfloat16)
        low = (values - high.astype(jnp.float32)).astype(jnp.bfloat16)
        both = lax.dot_general(
            jnp.concatenate([high, low], axis=0),
            spread,
            (((1,), (1,)), ((), ())),
            preferred_element_type=jnp.float32,
        )
        both = both[:height] + both[height:]
        total = both if total is None else total + both
    part_rows = height // len(outs)
    for part, out_ref in enumerate(outs):
        out_ref[...] = total[part * part_rows : (part + 1) * part_rows]


def assemble(block, arrived, holders, height, parts, block_size):
    chips = len(arrived)
    capacity = arrived[0].shape[2]
    piece = jax.ShapeDtypeStruct((height // parts, block_size), jnp.float32)
    return pl.pallas_call(
        functools.partial(assemble_kernel, block, block_size, height, chips),
        name="assemble",
        out_shape=[piece] * parts,
        in_specs=[in_vmem()] * (2 * chips),
        out_specs=[in_vmem()] * parts,
        compiler_params=params(24),
        cost_estimate=cost((ASSEMBLE, block, 0)),
    )(*arrived, *holders)


def stage_kernel(factor_ref, inverse_ref, *refs):
    outs, semaphores = refs[:-1], refs[-1]
    width = inverse_ref.shape[1]
    sources = [inverse_ref] + [
        factor_ref.at[:, pl.ds(block * width, width)] for block in range(1, len(outs))
    ]
    copies = [
        pltpu.make_async_copy(source, out, semaphores.at[place])
        for place, (source, out) in enumerate(zip(sources, outs))
    ]
    for copy in copies:
        copy.start()
    for copy in copies:
        copy.wait()


def stage(factor, inverse, count):
    depth, width = inverse.shape
    piece = jax.ShapeDtypeStruct((depth, width), inverse.dtype)
    return pl.pallas_call(
        stage_kernel,
        name="stage",
        out_shape=[piece] * count,
        in_specs=[in_hbm()] * 2,
        out_specs=[in_vmem()] * count,
        scratch_shapes=[pltpu.SemaphoreType.DMA((count,))],
        compiler_params=params(16),
        cost_estimate=cost((STAGE,)),
    )(factor, inverse)


def pick(group, part):
    return list(group) if part is None or len(group) == 1 else [group[part]]


def rows_of(refs, part, rows):
    if part is None:
        return refs[0][...] if len(refs) == 1 else jnp.concatenate([ref[...] for ref in refs], axis=0)
    if refs[0].shape[0] == rows:
        return refs[0][...]
    return refs[0][pl.ds(part * rows, rows), :]


def split(refs, counts):
    groups, refs = [], list(refs)
    for count in counts:
        groups.append(refs[:count])
        refs = refs[count:]
    return groups, refs


def station_kernel(station, part, counts, terms, has_next, held, *refs):
    groups, refs = split(refs, counts)
    right, inverse, rest = groups[0], groups[1][0], groups[2:]
    rows = right[0].shape[0] // PARTS
    ready = rest[terms + held :] if held else []
    solved_ref = refs[0].at[pl.ds(part * rows, rows)] if ready else refs[0]
    place = lax.axis_index("col")

    @pl.when(place == station)
    def _():
        reduced = rows_of(right, part, rows)
        for group in rest[:terms]:
            reduced = reduced - rows_of(group, part, rows)
        solved = contract(reduced.astype(jnp.bfloat16), inverse[...])
        solved_ref[...] = solved
        if has_next:
            onward = contract(solved.astype(jnp.bfloat16), rest[terms][0][...])
            for group in rest[terms + 1 :]:
                onward = onward + rows_of(group, part, rows)
            refs[1][...] = onward

    for earlier in range(held):

        @pl.when(place == earlier)
        def _(earlier=earlier):
            solved_ref[...] = rest[terms + earlier][0][...]

    for done, group in enumerate(ready):
        refs[0][pl.ds(done * rows, rows), :] = group[0][...]


def station_step(station, part, right, inverse, terms, factor, extra, held, ready):
    rows, width = right.shape[0] // PARTS, right.shape[1]
    groups = [[right], [inverse], *terms, *([] if factor is None else [[factor]]), *extra, *held, *ready]
    operands = [array for group in groups for array in group]
    piece = jax.ShapeDtypeStruct((rows * (len(ready) + 1), width), jnp.float32)
    count = 1 if factor is None else 2
    return pl.pallas_call(
        functools.partial(
            station_kernel, station, part, [len(group) for group in groups], len(terms),
            factor is not None, len(held),
        ),
        name="solve",
        out_shape=[piece] * count,
        in_specs=[in_vmem()] * len(operands),
        out_specs=[in_vmem()] * count,
        compiler_params=params(16),
        cost_estimate=cost((SOLVE, station, part)),
    )(*operands)


def onward_kernel(station, part, counts, *refs):
    groups, refs = split(refs, counts)

    @pl.when(lax.axis_index("col") == station)
    def _():
        rows = refs[0].shape[0]
        onward = contract(rows_of(groups[0], None, rows).astype(jnp.bfloat16), groups[1][0][...])
        for group in groups[2:]:
            onward = onward + rows_of(group, part, rows)
        refs[0][...] = onward


def onward_step(station, part, solved, factor, extra, key):
    rows, width = sum(array.shape[0] for array in solved), solved[0].shape[1]
    groups = [solved, [factor], *extra]
    operands = [array for group in groups for array in group]
    return pl.pallas_call(
        functools.partial(onward_kernel, station, part, [len(group) for group in groups]),
        name="onward",
        out_shape=jax.ShapeDtypeStruct((rows, width), jnp.float32),
        in_specs=[in_vmem()] * len(operands),
        out_specs=in_vmem(),
        compiler_params=params(16),
        cost_estimate=cost(key),
    )(*operands)


def local(desc_rows, upd_factor, update_index, owner_map, sep_rhs, factor_rows, diag_inverse):
    count = lax.axis_size("col")
    tiles = lax.axis_size("rhs")
    chips = tiles // CORES
    block_size = diag_inverse.shape[0]
    tile_rows = sep_rhs.shape[0]
    flow_parts = [FLOW_PARTS[min(block, len(FLOW_PARTS) - 1)] for block in range(count)]

    results, transfers, token = {}, {}, []
    arrived, partial, flow, sums, held, relayed, weights = {}, {}, {}, {}, {}, {}, {}
    risen = {block: {} for block in range(count)}

    def ordered(key, values):
        wanted = [array for group in values for array in group]
        earlier = list(token)
        for tie in TIES.get(key, ()):
            earlier += transfers.get(tie, [])
        if earlier:
            wanted = list(after(wanted, earlier))
        return split(wanted, [len(group) for group in values])[0]

    def moved(value, pairs, key):
        received = lax.ppermute(value, "col", pairs)
        transfers[key] = [received]
        return received

    def both_cores(mine, other):
        received = lax.ppermute(other, "rhs", [(p, p ^ 1) for p in range(tiles)])
        return [jnp.stack([mine[offset], received[offset]]) for offset in range(chips)]

    def exchange(pieces, gate, key):
        gates = transfers.get(gate) or results.get(gate)
        received = []
        for offset in range(1, chips):
            value = pieces[offset]
            if gates:
                value = after([value], [gates[(offset - 1) % len(gates)]])[0]
            pairs = [(p, p ^ (offset * CORES)) for p in range(tiles)]
            received.append(lax.ppermute(value, "rhs", pairs))
        transfers[key] = received
        arrived[key] = [pieces[0], *received]

    rows = desc_rows[0].reshape(tiles, tile_rows, block_size)
    wanted = [(0, part, PARTS) for part in range(PARTS)]
    wanted += [(block, 0, 1) for block in range(1, count)]
    first = payload(
        tuple(wanted[:1]), FIRST_MIB, owner_map, rows, upd_factor[0], update_index, count
    )
    payloads = [both_cores(*first[0])]
    token += [payloads[0][0]]

    hops = {0: []}
    stride = 1
    while stride < count:
        hops[0].append([(p + stride, p) for p in range(0, count - stride, 2 * stride)])
        stride *= 2
    for block in range(1, count):
        hops[block] = [[(p, p - 1)] for p in range(count - 1, block, -1)]

    def rest():
        late = ordered((PAYLOAD,), [[rows]])[0][0]
        pairs = payload(
            tuple(wanted[1:]), REST_MIB, owner_map, late, upd_factor[0], update_index, count
        )
        results[PAYLOAD] = pairs
        return pairs[0][:1]

    def load():
        groups = ordered((STAGE,), [[factor_rows], [diag_inverse]])
        got = stage(groups[0][0], groups[1][0], count)
        weights.update(enumerate(got))
        return got[:1]

    def send_block(block):
        gate = GATES[min(block, len(GATES) - 1)]
        exchange(payloads[PARTS + block - 1], gate, (PLANE, block, 0))

    def start_flow(block, part):
        flow[block, part] = [partial[block][part]]
        if hops[block]:
            flow[block, part].append(
                moved(partial[block][part], hops[block][0], (DOWN, block, 0, part))
            )

    def assemble_part(part):
        key = (ASSEMBLE, 0, part)
        values = ordered(key, [arrived[PLANE, 0, part], arrived[PLANE, 0, 0]])
        done = assemble(
            0, values[0], values[1], tile_rows // PARTS, flow_parts[0] // PARTS, block_size
        )
        results[key] = done
        if part == 0:
            for mine, other in results[PAYLOAD]:
                payloads.append(both_cores(mine, after([other], done[:1])[0]))
            send_block(1)
        if part + 1 < PARTS:
            exchange(payloads[part + 1], GATES[0], (PLANE, 0, part + 1))
        partial.setdefault(0, []).extend(done)
        for place in range(part * len(done), (part + 1) * len(done)):
            start_flow(0, place)
        return done

    def assemble_block(block):
        key = (ASSEMBLE, block, 0)
        values = ordered(key, [arrived[PLANE, block, 0], arrived[PLANE, 0, 0]])
        done = assemble(block, values[0], values[1], tile_rows, flow_parts[block], block_size)
        results[key] = partial[block] = done
        if block + 1 < count:
            send_block(block + 1)
        for part in range(flow_parts[block]):
            start_flow(block, part)
        return done

    def relay(block, hop, part):
        terms = flow[block, part]
        base = sums.get((block, part), terms[0])
        groups = ordered((RELAY, block, hop, part), [[base], [terms[-1]]])
        value = groups[0][0] + groups[1][0]
        received = moved(value, hops[block][hop], (DOWN, block, hop, part))
        if block == 0:
            flow[block, part] = [*terms, received]
            sums[block, part] = value
        else:
            flow[block, part] = [terms[0], received]
        return [value]

    def solve(station, part):
        last = station + 1 == count
        key = (SOLVE, station, part)
        terms = [[array] for array in flow[station, part if flow_parts[station] > 1 else 0]]
        terms += [[array] for array in risen[station].get(part, [])]
        extra = [] if last else [pick(partial[station + 1], part)]
        groups = ordered(key, [*terms, *extra])
        outs = station_step(
            station, part, sep_rhs, weights[0], groups[: len(terms)],
            None if last else weights[station + 1], groups[len(terms) :],
            [[held[part, k]] for k in range(station)] if last else [],
            [[held[p, station]] for p in range(part)] if last and part + 1 == PARTS else [],
        )
        held[part, station] = outs[0]
        if not last:
            received = moved(
                outs[1], [(station, station + 1)], (UP, station, station + 1, part)
            )
            risen[station + 1].setdefault(part, []).append(received)
        return outs[:1]

    def pass_on(station, block, part):
        key = (PASS, station, block, part)
        onto = block if station + 2 == block else station + 1
        extra = [pick(partial[block], part)]
        if (block, part) in relayed:
            extra.append([relayed.pop((block, part))])
        groups = ordered(key, [[held[part, station]], *extra])
        value = onward_step(station, part, groups[0], weights[block], groups[1:], key)
        received = moved(value, [(station, onto)], (UP, station, block, part))
        if onto == block:
            risen[block].setdefault(part, []).append(received)
        else:
            relayed[block, part] = received
        return [value]

    events = {(PAYLOAD,): rest, (STAGE,): load}
    requires = {}
    for part in range(PARTS):
        events[ASSEMBLE, 0, part] = functools.partial(assemble_part, part)
        requires[ASSEMBLE, 0, part] = [(ASSEMBLE, 0, p) for p in range(part)]
    for block in range(count):
        below = [(ASSEMBLE, b, 0) for b in range(1, min(block + 2, count))]
        if block:
            events[ASSEMBLE, block, 0] = functools.partial(assemble_block, block)
            requires[ASSEMBLE, block, 0] = below[: block - 1]
        for part in range(flow_parts[block]):
            own = below[:block] or [(ASSEMBLE, 0, part * PARTS // flow_parts[0])]
            for hop in range(1, len(hops[block])):
                events[RELAY, block, hop, part] = functools.partial(relay, block, hop, part)
                requires[RELAY, block, hop, part] = own + [
                    (RELAY, block, h, part) for h in range(1, hop)
                ]
        for part in range(PARTS):
            events[SOLVE, block, part] = functools.partial(solve, block, part)
            flowing = part if flow_parts[block] > 1 else 0
            requires[SOLVE, block, part] = [
                (STAGE,),
                *below,
                *([] if block else [(ASSEMBLE, 0, p) for p in range(part + 1)]),
                *[(RELAY, block, hop, flowing) for hop in range(1, len(hops[block]))],
                *[(SOLVE, k, p) for k in range(block) for p in range(part + 1)],
                *[(SOLVE, block, p) for p in range(part)],
                *[(PASS, k, block, part) for k in range(block - 1)],
            ]
            for k in range(block - 1):
                events[PASS, k, block, part] = functools.partial(pass_on, k, block, part)
                requires[PASS, k, block, part] = [
                    *below[:block],
                    *[(SOLVE, k, p) for p in range(part + 1)],
                    *[(PASS, e, block, part) for e in range(k)],
                ]

    def run(key):
        if key in token_of or key not in events:
            return
        for earlier in requires.get(key, ()):
            run(earlier)
        token_of[key] = events[key]()
        token[:] = token_of[key][:1]

    token_of = {}
    exchange(payloads[0], None, (PLANE, 0, 0))
    for key in ((PAYLOAD,), (ASSEMBLE, 0, 0), *ORDER):
        run(key)
    for part in range(PARTS):
        run((SOLVE, count - 1, part))
    return held[PARTS - 1, count - 1]


def solution(mesh):
    placed = (
        P(("col", "rhs"), None, None),
        P(("col", "rhs"), None, None),
        P(("col", "rhs"), None),
        P(("col", "rhs"), None),
        P("rhs", "col"),
        P("col", None),
        P("col", None),
    )
    return jax.shard_map(
        local, mesh=mesh, in_specs=placed, out_specs=P("rhs", "col"), check_vma=False
    )
```
